32 devices in a mesh: grp: 2 (over y), dp: 4 (over z), mod: 2 (over x), rep: 2 (over core).
Axes of the slice: x: 2, y: 2, z: 4, core: 2. Of those that a mesh axis runs over, the one named last changes fastest.
Arguments:
- activations: bfloat16 [2, 8, 1024, 4096], P('mod', ('grp', 'dp'), 'rep'), parts along dimension 1, may hold values from -6 to 6
- out_grads: bfloat16 [2, 8, 1024, 4096], P('mod', ('grp', 'dp'), 'rep'), parts along dimension 1, may hold values from -0.1875 to 0.1875
- proj_in: bfloat16 [2, 32, 4096], P('mod'), may hold values from -0.09375 to 0.09375
- proj_out: bfloat16 [2, 32, 4096], P('mod'), may hold values from -0.09375 to 0.09375
- seq_lengths: int32 [8], P(('grp', 'dp')), parts along dimension 0, may hold values from 256 to 1024, as said below
- fisher_prior: float32 [2, 16, 1024, 1024], P('mod', ('grp', 'dp', 'rep')), parts along dimension 1, may hold values from -160 to 160, as said below
- query_grads: bfloat16 [2, 2, 512, 1024], P('mod', 'rep', 'dp'), may hold values from -32 to 32
Outputs:
- influence: float32 [8, 1024], P(('grp', 'dp'), 'rep'), parts along dimension 0
The draws below stay inside these ranges and needn't reach their ends.
There are 2 independent parts, one for each index of `grp`. The reference program is written for one: setup_inputs(seed, part) draws one part's arguments, and reference() takes and returns one part's arrays. A program takes and returns all parts, laid end to end along the dimension named above; an argument that names none is the same for every part. Nothing has to cross between parts.
Inputs may be any that keep to these rules, and one draw needn't show every extreme that they name: `seq_lengths`: tokens of a sequence at positions from its length on do not count; in every draw some sequence has all 1024 tokens. `fisher_prior`: each partial is symmetric positive definite.
All inputs are finite; a program needn't handle non-finite values.
Results may differ from the reference program's by a relative error of at most 0.0003.
Values may be sent and summed in bfloat16 or wider, within the bound.
No kernel may reach another device: no remote copies, remote signals or barrier semaphores. Data moves between devices by JAX's collectives and lax.ppermute only.
A program may use at most 128 MiB of HBM per device.

```python
import jax
import jax.numpy as jnp
from jax import lax

D = 4096
RANK = 32
LEN = 1024
R = 1024
TRAIN = 4
MODULES = 2
SHARDS = 8
QB = 512
QBLOCKS = 2
QUERIES = 1024


private_frac = 0.05


def draw_seq_lengths(key, part):
    key = jax.random.fold_in(key, 23)
    first_key, second_key = jax.random.split(key)
    drawn = jax.random.randint(first_key, (TRAIN,), LEN // 4, LEN + 1)
    spot = jax.random.randint(second_key, (), 0, TRAIN)
    return jnp.where(jnp.arange(TRAIN) == spot, LEN, drawn).astype(jnp.int32)


def draw_fisher_prior(key, part):
    key = jax.random.fold_in(key, 11)
    diag_key, mix_key, row_key, weight_key, shard_key = jax.random.split(key, 5)
    order = jnp.arange(R, dtype=jnp.float32) + 1.0
    narrow = R // 4
    mixing = jnp.clip(jax.random.normal(mix_key, (MODULES, R, R), jnp.float32), -2.0, 2.0)
    shard_mix = jnp.clip(jax.random.normal(shard_key, (MODULES, SHARDS, R, narrow), jnp.float32), -2.0, 2.0)
    spectrum = 1.0 / order
    row_scale = jnp.sqrt(jnp.exp(jax.random.uniform(row_key, (MODULES, R), jnp.float32, 0.0, jnp.log(10.0))))
    weights = jnp.exp(jax.random.uniform(weight_key, (MODULES, SHARDS), jnp.float32, 0.0, jnp.log(3.0)))
    diagonal = jnp.exp(jax.random.uniform(diag_key, (MODULES, SHARDS, R), jnp.float32, jnp.log(0.005), jnp.log(0.05)))
    spectrum = spectrum / jnp.sum(spectrum)
    scaled = mixing * row_scale[:, :, None]
    common = jnp.einsum('mri,msi->mrs', scaled * spectrum[None, None, :], scaled, precision=lax.Precision.HIGHEST)
    common = 0.5 * (common + jnp.swapaxes(common, 1, 2))
    private_part = jnp.einsum('mkrp,mksp->mkrs', shard_mix, shard_mix, precision=lax.Precision.HIGHEST)
    private_part = 0.5 * private_frac / R * (private_part + jnp.swapaxes(private_part, 2, 3))
    identity = jnp.eye(R, dtype=jnp.float32)
    return diagonal[..., :, None] * identity + weights[:, :, None, None] * common[:, None, :, :] + private_part


def block_levels(own_key, dims, shards, smallest, top_value):
    gain = 1.0
    for position, blocks in shards:
        heights = jax.random.uniform(jax.random.fold_in(jax.random.fold_in(own_key, 6), position), (blocks,), jnp.float32, smallest / len(shards), top_value / len(shards))
        gain = gain * jnp.repeat(jnp.exp(heights), dims[position] // blocks).reshape((-1,) + (1,) * (len(dims) - 1 - position))
    return gain


def centred(rng, extent, spread, limit, cuts=(), kind=jnp.bfloat16):
    array = spread * jax.random.normal(rng, extent, jnp.float32)
    if cuts:
        array = array * block_levels(rng, extent, cuts, -0.22, 0.18)
    return jnp.clip(array, -limit, limit).astype(kind)


def setup_inputs(seed: int = 0, part: int = 0) -> dict:
    arg_keys = jax.random.split(jax.random.key(seed), 8)
    part_splits = jax.random.split(jax.random.fold_in(arg_keys[7], part), 8)
    activations = centred(part_splits[0], (MODULES, TRAIN, LEN, D), 1.0, 6.0, ((0, 2), (1, 4), (2, 2)))
    out_grads = centred(part_splits[1], (MODULES, TRAIN, LEN, D), 0.03125, 0.1875, ((0, 2), (1, 4), (2, 2)))
    proj_in = centred(arg_keys[2], (MODULES, RANK, D), D ** -0.5, 0.09375, ((0, 2),))
    proj_out = centred(arg_keys[3], (MODULES, RANK, D), D ** -0.5, 0.09375, ((0, 2),))
    seq_lengths = draw_seq_lengths(jax.random.fold_in(jax.random.fold_in(arg_keys[7], part), 71), part)
    fisher_prior = draw_fisher_prior(jax.random.fold_in(jax.random.fold_in(arg_keys[7], part), 71), part)
    query_grads = centred(arg_keys[6], (MODULES, QBLOCKS, QB, R), 6.0, 32.0, ((0, 2), (1, 2), (2, 4)))
    return dict(activations=activations, out_grads=out_grads, proj_in=proj_in, proj_out=proj_out, seq_lengths=seq_lengths, fisher_prior=fisher_prior, query_grads=query_grads)


damping_frac = 0.01

def project_vectors(activations, out_grads, proj_in, proj_out, keeper):
    seq_count, tok_count, feat_width = activations.shape
    rank_in = proj_in.shape[0]
    rank_out = proj_out.shape[0]
    in_side = jnp.dot(activations.reshape(seq_count * tok_count, feat_width).astype(jnp.float32), proj_in.T.astype(jnp.float32), preferred_element_type=jnp.float32)
    out_side = jnp.dot(out_grads.reshape(seq_count * tok_count, feat_width).astype(jnp.float32), proj_out.T.astype(jnp.float32), preferred_element_type=jnp.float32)
    in_side = in_side.reshape(seq_count, tok_count, rank_in)
    out_side = out_side.reshape(seq_count, tok_count, rank_out) * keeper[:, :, None]
    outer_sum = jnp.einsum('sto,sti->soi', out_side, in_side, precision=lax.Precision.HIGHEST)
    return outer_sum.reshape(seq_count, rank_out * rank_in)

def reference(activations, out_grads, proj_in, proj_out, seq_lengths, fisher_prior, query_grads):
    positions = jnp.arange(LEN, dtype=jnp.int32)
    keeper = (positions[None, :] < seq_lengths[:, None]).astype(jnp.float32)
    query_flat = query_grads.reshape(MODULES, QUERIES, RANK * RANK)
    influence = jnp.zeros((TRAIN, QUERIES), jnp.float32)
    for module in range(MODULES):
        vectors = project_vectors(activations[module], out_grads[module], proj_in[module], proj_out[module], keeper)
        fisher = jnp.sum(fisher_prior[module], axis=0) + jnp.dot(vectors.T, vectors, precision=lax.Precision.HIGHEST)
        proj_dim = fisher.shape[0]
        damping = damping_frac * jnp.trace(fisher) / proj_dim
        system = fisher + damping * jnp.eye(proj_dim, dtype=jnp.float32)
        factor = jnp.linalg.cholesky(system)
        solved = jax.scipy.linalg.cho_solve((factor, True), query_flat[module].astype(jnp.float32).T)
        influence = influence + jnp.dot(vectors, solved, precision=lax.Precision.HIGHEST)
    return influence
```

```python
import functools

import jax
import jax.numpy as jnp
from jax import lax
from jax.experimental import pallas as pl
from jax.experimental.pallas import tpu as pltpu
from jax.sharding import PartitionSpec as P

damping_frac = 0.01
NB = 128
LANES = 128
SUB = 8
HIGH = lax.Precision.HIGHEST


def iota(shape, dim):
    return lax.broadcasted_iota(jnp.int32, shape, dim)


def dot(a, b, dims, precision=HIGH):
    return lax.dot_general(
        a, b, (dims, ((), ())), precision=precision, preferred_element_type=jnp.float32
    )


def project_kernel(steps, rank, place_ref, act_ref, grad_ref, pin_ref, pout_ref, prior_ref, out_ref, pin4, acc, tr):
    step = pl.program_id(0)
    tile = act_ref.shape[2]
    fold = LANES // rank

    @pl.when(step == 0)
    def _():
        for r in range(fold):
            pin4[r * rank : (r + 1) * rank, :] = pin_ref[0]
        acc[...] = jnp.zeros_like(acc)
        tr[...] = jnp.zeros_like(tr)

    in_side = dot(act_ref[0, 0], pin4[...], ((1,), (1,)), None)
    out_side = dot(grad_ref[0, 0], pout_ref[0], ((1,), (1,)), None)
    token = place_ref[0] + step * tile + iota(out_side.shape, 0)
    out_side = jnp.where(token < place_ref[1], out_side, 0.0)
    acc[...] += dot(out_side, in_side, ((0,), (0,)))
    block = prior_ref[0, 0]
    on_diag = iota(block.shape, 0) == iota(block.shape, 1)
    block = jnp.where(on_diag, block, 0.0)
    line = jnp.sum(block, axis=0, keepdims=True)
    tr[0:1, :] += sum(line[:, c : c + LANES] for c in range(0, block.shape[1], LANES))

    @pl.when(step == steps - 1)
    def _():
        rows = rank // fold
        o = iota((rank, LANES), 0)
        lane = iota((rank, LANES), 1)
        kept = jnp.where(lax.rem(o, fold) == lane // rank, acc[...], 0.0)
        pick = (iota((rows, rank), 1) // fold == iota((rows, rank), 0)).astype(jnp.float32)
        out_ref[0:rows, :] = dot(pick, kept, ((1,), (0,)))
        out_ref[rows:, :] = tr[...]


def project(place, activations, out_grads, proj_in, proj_out, fisher_prior):
    steps = 4
    tok, width = activations.shape[2:]
    rank = proj_in.shape[1]
    size = fisher_prior.shape[2]
    tile, blk = tok // steps, size // steps
    rows = size // LANES
    return pl.pallas_call(
        functools.partial(project_kernel, steps, rank),
        grid=(steps,),
        in_specs=[
            pl.BlockSpec(memory_space=pltpu.SMEM),
            pl.BlockSpec((1, 1, tile, width), lambda i: (0, 0, i, 0)),
            pl.BlockSpec((1, 1, tile, width), lambda i: (0, 0, i, 0)),
            pl.BlockSpec((1, rank, width), lambda i: (0, 0, 0)),
            pl.BlockSpec((1, rank, width), lambda i: (0, 0, 0)),
            pl.BlockSpec((1, 1, blk, blk), lambda i: (0, 0, i, i)),
        ],
        out_specs=pl.BlockSpec((rows + SUB, LANES), lambda i: (0, 0)),
        out_shape=jax.ShapeDtypeStruct((rows + SUB, LANES), jnp.float32),
        scratch_shapes=[
            pltpu.VMEM((LANES, width), jnp.bfloat16),
            pltpu.VMEM((rank, LANES), jnp.float32),
            pltpu.VMEM((SUB, LANES), jnp.float32),
        ],
        compiler_params=pltpu.CompilerParams(vmem_limit_bytes=32 << 20),
        name="project",
    )(place, activations, out_grads, proj_in, proj_out, fisher_prior)


def reciprocal(p):
    r = pl.reciprocal(p, approx=True)
    r = r * (2.0 - p * r)
    return r * (2.0 - p * r)


def spread(x, k):
    return jnp.broadcast_to(x[k : k + 1, :], x.shape)


def lanes_of(x, k):
    return jnp.broadcast_to(x[:, k : k + 1], x.shape)


def eliminate(rows):
    groups = len(rows)
    rows = list(rows)
    sub = iota((SUB, LANES), 0)
    lane = iota((SUB, LANES), 1)
    lower, scaled = [], []
    for g in range(groups):
        first = g * SUB
        here = (lane >= first) & (lane < first + SUB)
        unit = (lane - first == sub).astype(jnp.float32)
        own = rows[g]
        cols = [lanes_of(own, first + j) for j in range(SUB)]
        work = jnp.where(here, unit, own)
        lower.append(jnp.where(lane < first + SUB, work, 0.0))
        for k in range(SUB):
            pivot_row = sub == k
            r = reciprocal(spread(cols[k], k))
            c = jnp.where(pivot_row, -1.0, cols[k])
            for j in range(k + 1, SUB):
                cols[j] = jnp.where(pivot_row, 0.0, cols[j]) - (c * spread(cols[j], k)) * r
            work = jnp.where(pivot_row, 0.0, work) - (c * spread(work, k)) * r
        scaled.append(jnp.where(lane < first + SUB, work, 0.0))
        if g + 1 < groups:
            picks = [spread(work, j) for j in range(SUB)]
            for h in range(g + 1, groups):
                x = rows[h]
                terms = [lanes_of(x, first + j) * picks[j] for j in range(SUB)]
                while len(terms) > 1:
                    terms = [terms[i] + terms[i + 1] for i in range(0, len(terms), 2)]
                rows[h] = jnp.where(here, 0.0, x) - terms[0]
    return lower, scaled


def factor_kernel(size, seqs, own_ref, parts_ref, *refs):
    blocks = size // NB
    chunks, (query_ref, out_ref, a, ef, vec, rhs) = refs[:-6], refs[-6:]
    reps = parts_ref.shape[1]
    for b in range(blocks):
        piece = parts_ref[:, 0, b, :]
        for r in range(1, reps):
            piece = piece + parts_ref[:, r, b, :]
        vec[:, b * NB : (b + 1) * NB] = piece
    v = vec[...]
    trace = jnp.sum(parts_ref[:, :, blocks:, :]) + jnp.sum(v * v)
    damping = damping_frac * trace / size
    mine = iota((seqs, size), 0) == own_ref[0]
    rhs[...] = jnp.broadcast_to(jnp.sum(jnp.where(mine, v, 0.0), axis=0, keepdims=True), rhs.shape)
    done = 0
    for chunk in chunks:
        tall, wide = chunk.shape
        outer = dot(vec[:, done : done + tall], vec[:, 0:wide], ((0,), (0,)))
        eye = iota((tall, wide), 0) + done == iota((tall, wide), 1)
        a[done : done + tall, 0:wide] = chunk[...] + outer + jnp.where(eye, damping, 0.0)
        done += tall

    for k in range(blocks):
        at, end = k * NB, (k + 1) * NB
        low, scl = eliminate([a[at + i * SUB : at + (i + 1) * SUB, at:end] for i in range(NB // SUB)])
        for i in range(NB // SUB):
            ef[k, i * SUB : (i + 1) * SUB, :] = low[i]
            ef[k, NB + i * SUB : NB + (i + 1) * SUB, :] = scl[i]
        both = ef[k]
        x = dot(rhs[:, at:end], both, ((1,), (1,)))
        rhs[:, at:end] = x[:, NB:]
        if end < size:
            y = dot(a[end:, at:end], both, ((1,), (1,)))
            a[end:, at:end] = y[:, NB:]
            left = y[:, :NB]
            rhs[:, end:] -= dot(x[:, NB:], left, ((1,), (1,)))
            for j in range(k + 1, blocks):
                top = j * NB
                a[top:, top : top + NB] -= dot(
                    a[top:, at:end], left[top - end : top - end + NB], ((1,), (1,))
                )
    for k in range(blocks - 1, -1, -1):
        at, end = k * NB, (k + 1) * NB
        z = dot(rhs[:, at:end], ef[k, 0:NB, :], ((1,), (0,)))
        rhs[:, at:end] = z
        if k:
            rhs[:, 0:at] -= dot(z, a[at:end, 0:at], ((1,), (0,)))
    out_ref[...] = dot(rhs[...], query_ref[...].astype(jnp.float32), ((1,), (1,)))


def factor(own, parts, chunks, queries):
    seqs = parts.shape[0]
    count, size = queries.shape
    blocks = size // NB
    vmem = pl.BlockSpec(memory_space=pltpu.VMEM)
    return pl.pallas_call(
        functools.partial(factor_kernel, size, seqs),
        in_specs=[pl.BlockSpec(memory_space=pltpu.SMEM)] + [vmem] * (2 + len(chunks)),
        out_specs=vmem,
        out_shape=jax.ShapeDtypeStruct((SUB, count), jnp.float32),
        scratch_shapes=[
            pltpu.VMEM((size, size), jnp.float32),
            pltpu.VMEM((blocks, 2 * NB, NB), jnp.float32),
            pltpu.VMEM((seqs, size), jnp.float32),
            pltpu.VMEM((SUB, size), jnp.float32),
        ],
        compiler_params=pltpu.CompilerParams(vmem_limit_bytes=48 << 20),
        name="factor",
    )(own, parts, *chunks, queries)


def body(activations, out_grads, proj_in, proj_out, seq_lengths, fisher_prior, query_grads):
    tok_half = activations.shape[2]
    size = fisher_prior.shape[2]
    place = jnp.stack([lax.axis_index("rep") * tok_half, seq_lengths[0]]).astype(jnp.int32)
    part = project(place, activations, out_grads, proj_in, proj_out, fisher_prior)
    wide = size // 4
    chunks = [
        lax.psum(fisher_prior[0, 0, c * wide : (c + 1) * wide, 0 : (c + 1) * wide], ("dp", "rep"))
        for c in range(4)
    ]
    parts = lax.all_gather(part, ("dp", "rep"))
    parts = parts.reshape((-1, lax.axis_size("rep")) + part.shape)
    queries = lax.all_gather(query_grads[0, 0], "dp", axis=0, tiled=True)
    own = lax.axis_index("dp").astype(jnp.int32).reshape(1)
    scores = factor(own, parts, chunks, queries)
    return lax.psum(scores[0:1], "mod")


def solution(mesh):
    placed = (
        P("mod", ("grp", "dp"), "rep", None),
        P("mod", ("grp", "dp"), "rep", None),
        P("mod", None, None),
        P("mod", None, None),
        P(("grp", "dp")),
        P("mod", ("grp", "dp", "rep"), None, None),
        P("mod", "rep", "dp", None),
    )
    return jax.shard_map(
        body, mesh=mesh, in_specs=placed, out_specs=P(("grp", "dp"), "rep"), check_vma=False
    )
```

```python
import functools

import jax
import jax.numpy as jnp
from jax import lax
from jax.experimental import pallas as pl
from jax.experimental.pallas import tpu as pltpu
from jax.sharding import PartitionSpec as P

damping_frac = 0.01
NB = 128
LANES = 128
SUB = 8
CHUNKS = 4
HIGH = lax.Precision.HIGHEST


def iota(shape, dim):
    return lax.broadcasted_iota(jnp.int32, shape, dim)


def dot(a, b, dims, precision=HIGH):
    return lax.dot_general(
        a, b, (dims, ((), ())), precision=precision, preferred_element_type=jnp.float32
    )


def split(x):
    one = x.astype(jnp.bfloat16)
    x = x - one.astype(jnp.float32)
    two = x.astype(jnp.bfloat16)
    three = (x - two.astype(jnp.float32)).astype(jnp.bfloat16)
    return one, two, three


def left_terms(x):
    one, two, three = split(x)
    return jnp.concatenate([one, one, two, two, one, three], axis=1)


def right_terms(x):
    one, two, three = split(x)
    return jnp.concatenate([one, two, one, two, three, one], axis=1)


def by_rows(a, b):
    return dot(a, b, ((1,), (1,)), None)


def project_kernel(steps, rank, place_ref, act_ref, grad_ref, pin_ref, pout_ref, prior_ref, out_ref, pin4, acc, tr):
    step = pl.program_id(0)
    tile = act_ref.shape[2]
    fold = LANES // rank

    @pl.when(step == 0)
    def _():
        for r in range(fold):
            pin4[r * rank : (r + 1) * rank, :] = pin_ref[0]
        acc[...] = jnp.zeros_like(acc)
        tr[...] = jnp.zeros_like(tr)

    in_side = dot(act_ref[0, 0], pin4[...], ((1,), (1,)), None)
    out_side = dot(grad_ref[0, 0], pout_ref[0], ((1,), (1,)), None)
    token = place_ref[0] + step * tile + iota(out_side.shape, 0)
    out_side = jnp.where(token < place_ref[1], out_side, 0.0)
    acc[...] += dot(out_side, in_side, ((0,), (0,)))
    block = prior_ref[0, 0]
    on_diag = iota(block.shape, 0) == iota(block.shape, 1)
    block = jnp.where(on_diag, block, 0.0)
    line = jnp.sum(block, axis=0, keepdims=True)
    tr[0:1, :] += sum(line[:, c : c + LANES] for c in range(0, block.shape[1], LANES))

    @pl.when(step == steps - 1)
    def _():
        rows = rank // fold
        o = iota((rank, LANES), 0)
        lane = iota((rank, LANES), 1)
        kept = jnp.where(lax.rem(o, fold) == lane // rank, acc[...], 0.0)
        pick = (iota((rows, rank), 1) // fold == iota((rows, rank), 0)).astype(jnp.float32)
        vector = dot(pick, kept, ((1,), (0,)))
        for s in range(out_ref.shape[0] - 1):
            out_ref[s] = jnp.where(place_ref[2] == s, vector, 0.0)
        out_ref[out_ref.shape[0] - 1] = tr[...]


def project(place, seqs, activations, out_grads, proj_in, proj_out, fisher_prior):
    steps = 4
    tok, width = activations.shape[2:]
    rank = proj_in.shape[1]
    size = fisher_prior.shape[2]
    tile, blk = tok // steps, size // steps
    rows = size // LANES
    return pl.pallas_call(
        functools.partial(project_kernel, steps, rank),
        grid=(steps,),
        in_specs=[
            pl.BlockSpec(memory_space=pltpu.SMEM),
            pl.BlockSpec((1, 1, tile, width), lambda i: (0, 0, i, 0)),
            pl.BlockSpec((1, 1, tile, width), lambda i: (0, 0, i, 0)),
            pl.BlockSpec((1, rank, width), lambda i: (0, 0, 0)),
            pl.BlockSpec((1, rank, width), lambda i: (0, 0, 0)),
            pl.BlockSpec((1, 1, blk, blk), lambda i: (0, 0, i, i)),
        ],
        out_specs=pl.BlockSpec((seqs + 1, rows, LANES), lambda i: (0, 0, 0)),
        out_shape=jax.ShapeDtypeStruct((seqs + 1, rows, LANES), jnp.float32),
        scratch_shapes=[
            pltpu.VMEM((LANES, width), jnp.bfloat16),
            pltpu.VMEM((rank, LANES), jnp.float32),
            pltpu.VMEM((rows, LANES), jnp.float32),
        ],
        compiler_params=pltpu.CompilerParams(vmem_limit_bytes=60 << 20),
        name="project",
    )(place, activations, out_grads, proj_in, proj_out, fisher_prior)


def reciprocal(p):
    r = pl.reciprocal(p, approx=True)
    return r * (2.0 - p * r)


def spread(x, k):
    return jnp.broadcast_to(x[k : k + 1, :], x.shape)


def lanes_of(x, k):
    return jnp.broadcast_to(x[:, k : k + 1], x.shape)


def solve_group(s, w):
    s = [list(row) for row in s]
    w = list(w)
    pairs = []
    for k in range(0, SUB, 2):
        a, b, c = s[k][k], s[k + 1][k], s[k + 1][k + 1]
        r = reciprocal(a * c - b * b)
        rest = range(k + 2, SUB)
        m = {i: s[i][k] * c - s[i][k + 1] * b for i in rest}
        n = {i: s[i][k + 1] * a - s[i][k] * b for i in rest}
        for i in rest:
            for j in range(k + 2, i + 1):
                s[i][j] = s[i][j] - (m[i] * s[j][k] + n[i] * s[j][k + 1]) * r
        m = {i: m[i] * r for i in rest}
        n = {i: n[i] * r for i in rest}
        for i in rest:
            w[i] = w[i] - (m[i] * w[k] + n[i] * w[k + 1])
        u, v = w[k], w[k + 1]
        w[k], w[k + 1] = (c * u - b * v) * r, (a * v - b * u) * r
        pairs.append((m, n))
    for k in range(SUB - 4, -1, -2):
        m, n = pairs[k // 2]
        for i in range(k + 2, SUB):
            w[k] = w[k] - m[i] * w[i]
            w[k + 1] = w[k + 1] - n[i] * w[i]
    return w


def eliminate(rows):
    groups = len(rows)
    rows = list(rows)
    sub = iota((SUB, LANES), 0)
    lane = iota((SUB, LANES), 1)
    lower, scaled = [], []
    for g in range(groups):
        first = g * SUB
        here = (lane >= first) & (lane < first + SUB)
        unit = (lane - first == sub).astype(jnp.float32)
        own = rows[g]
        cols = [lanes_of(own, first + j) for j in range(SUB)]
        s = [[spread(cols[j], i) for j in range(i + 1)] for i in range(SUB)]
        work = jnp.where(here, unit, own)
        lower.append(jnp.where(lane < first + SUB, work, 0.0))
        picks = solve_group(s, [spread(work, i) for i in range(SUB)])
        work = picks[0]
        for i in range(1, SUB):
            work = jnp.where(sub == i, picks[i], work)
        scaled.append(jnp.where(lane < first + SUB, work, 0.0))
        for h in range(g + 1, groups):
            x = rows[h]
            terms = [lanes_of(x, first + j) * picks[j] for j in range(SUB)]
            while len(terms) > 1:
                terms = [terms[i] + terms[i + 1] for i in range(0, len(terms), 2)]
            rows[h] = jnp.where(here, 0.0, x) - terms[0]
    return lower, scaled


def factor_kernel(size, place_ref, parts_ref, *refs):
    blocks = size // NB
    halves, (out_ref, a, ef, vec, left, right) = refs[: 2 * CHUNKS], refs[2 * CHUNKS :]
    seqs = parts_ref.shape[0] - 1
    padded = vec.shape[0]
    if padded > seqs:
        vec[seqs:, :] = jnp.zeros((padded - seqs, size), jnp.float32)
    for b in range(blocks):
        vec[0:seqs, b * NB : (b + 1) * NB] = parts_ref[0:seqs, b, :]
    v = vec[...]
    trace = jnp.sum(parts_ref[seqs]) + jnp.sum(v * v)
    scale = size / jnp.broadcast_to(trace, (1, LANES))
    scale_row = jnp.concatenate([scale] * blocks, axis=1)
    one, two, three = split(v)
    outer_left = jnp.concatenate([one, one, two, two, one, three], axis=0)
    outer_right = jnp.concatenate([one, two, one, two, three, one], axis=0)
    rep = place_ref[0]
    half = size // CHUNKS // 2
    for c in range(CHUNKS):
        top, wide = 2 * c * half, 2 * (c + 1) * half
        a[pl.ds(top + rep * half, half), 0:wide] = halves[2 * c][...]
        a[pl.ds(top + (1 - rep) * half, half), 0:wide] = halves[2 * c + 1][...]
        outer = dot(outer_left[:, top:wide], outer_right[:, 0:wide], ((0,), (0,)), None)
        eye = iota((2 * half, wide), 0) + top == iota((2 * half, wide), 1)
        a[top:wide, 0:wide] = (a[top:wide, 0:wide] + outer) * scale_row[:, 0:wide] + jnp.where(
            eye, damping_frac, 0.0
        )
    a[size:, :] = v

    for k in range(blocks):
        at, end = k * NB, (k + 1) * NB
        low, scl = eliminate([a[at + i * SUB : at + (i + 1) * SUB, at:end] for i in range(NB // SUB)])
        for i in range(NB // SUB):
            ef[k, i * SUB : (i + 1) * SUB, :] = low[i]
            ef[k, NB + i * SUB : NB + (i + 1) * SUB, :] = scl[i]
        y = by_rows(left_terms(a[end:, at:end]), right_terms(ef[k]))
        a[end:, at:end] = y[:, NB:]
        if end < size:
            left[end:, :] = left_terms(y[:, NB:])
            right[end:, :] = right_terms(y[: size - end, :NB])
            for top in range(end, size, 2 * NB):
                stop = min(top + 2 * NB, size)
                a[top:, top:stop] -= by_rows(left[top:, :], right[top:stop, :])
    for k in range(blocks - 1, -1, -1):
        at, end = k * NB, (k + 1) * NB
        z = dot(a[size:, at:end], ef[k, 0:NB, :], ((1,), (0,)))
        a[size:, at:end] = z
        if k:
            a[size:, 0:at] -= dot(z, a[at:end, 0:at], ((1,), (0,)))
    out_ref[...] = a[size:, :] * scale_row


def factor(place, parts, halves):
    seqs = parts.shape[0] - 1
    size = halves[-1].shape[1]
    blocks = size // NB
    padded = -(-seqs // SUB) * SUB
    vmem = pl.BlockSpec(memory_space=pltpu.VMEM)
    return pl.pallas_call(
        functools.partial(factor_kernel, size),
        in_specs=[pl.BlockSpec(memory_space=pltpu.SMEM)] + [vmem] * (1 + len(halves)),
        out_specs=vmem,
        out_shape=jax.ShapeDtypeStruct((padded, size), jnp.float32),
        scratch_shapes=[
            pltpu.VMEM((size + padded, size), jnp.float32),
            pltpu.VMEM((blocks, 2 * NB, NB), jnp.float32),
            pltpu.VMEM((padded, size), jnp.float32),
            pltpu.VMEM((size + padded, 6 * NB), jnp.bfloat16),
            pltpu.VMEM((size, 6 * NB), jnp.bfloat16),
        ],
        compiler_params=pltpu.CompilerParams(vmem_limit_bytes=44 << 20),
        name="factor",
    )(place, parts, *halves)


def score_kernel(solved_ref, query_ref, out_ref):
    rows = solved_ref.shape[0]
    terms = by_rows(jnp.concatenate(split(solved_ref[...]), axis=0), query_ref[...])
    out_ref[...] = terms[0:rows] + terms[rows : 2 * rows] + terms[2 * rows :]


def score(solved, queries):
    vmem = pl.BlockSpec(memory_space=pltpu.VMEM)
    return pl.pallas_call(
        score_kernel,
        in_specs=[vmem, vmem],
        out_specs=vmem,
        out_shape=jax.ShapeDtypeStruct((solved.shape[0], queries.shape[0]), jnp.float32),
        name="score",
    )(solved, queries)


def sum_to_middle(x):
    n = lax.axis_size("dp")
    for s in range(n // 2 - 1):
        x = x + lax.ppermute(x, "dp", [(s, s + 1), (n - 1 - s, n - 2 - s)])
    if n > 1:
        m = n // 2
        x = x + lax.ppermute(x, "dp", [(m - 1, m), (m, m - 1)])
    return x


def from_middle(x):
    n = lax.axis_size("dp")
    here = lax.axis_index("dp")
    for s in range(n // 2 - 2, -1, -1):
        got = lax.ppermute(x, "dp", [(s + 1, s), (n - 2 - s, n - 1 - s)])
        x = jnp.where((here == s) | (here == n - 1 - s), got, x)
    return x


SWAP = [(0, 1), (1, 0)]


def body(activations, out_grads, proj_in, proj_out, seq_lengths, fisher_prior, query_grads):
    tok_half = activations.shape[2]
    size = fisher_prior.shape[2]
    rep, dp = lax.axis_index("rep"), lax.axis_index("dp")
    half = size // CHUNKS // 2
    sums = []
    for c in range(CHUNKS):
        top, wide = 2 * c * half, 2 * (c + 1) * half
        other = lax.dynamic_slice(fisher_prior[0, 0], (top + (1 - rep) * half, 0), (half, wide))
        own = lax.dynamic_slice(fisher_prior[0, 0], (top + rep * half, 0), (half, wide))
        sums.append(own + lax.ppermute(other, "rep", SWAP))
    place = jnp.stack([rep * tok_half, seq_lengths[0], dp]).astype(jnp.int32)
    seqs = lax.axis_size("dp")
    part = project(place, seqs, activations, out_grads, proj_in, proj_out, fisher_prior)
    halves = []
    for c in range(CHUNKS):
        x = sum_to_middle(sums[c])
        halves += [x, lax.ppermute(x, "rep", SWAP)]
    part = part + lax.ppermute(part, "rep", SWAP)
    part = sum_to_middle(part)
    query, halves = lax.optimization_barrier((query_grads[0, 0], halves))
    queries = lax.all_gather(query, "dp", axis=0, tiled=True)
    solved = factor(rep.astype(jnp.int32).reshape(1), part, halves)
    scores = from_middle(lax.psum(score(solved, queries), "mod"))
    return lax.dynamic_slice(scores, (dp, 0), (1, scores.shape[1]))


def solution(mesh):
    placed = (
        P("mod", ("grp", "dp"), "rep", None),
        P("mod", ("grp", "dp"), "rep", None),
        P("mod", None, None),
        P("mod", None, None),
        P(("grp", "dp")),
        P("mod", ("grp", "dp", "rep"), None, None),
        P("mod", "rep", "dp", None),
    )
    return jax.shard_map(
        body, mesh=mesh, in_specs=placed, out_specs=P(("grp", "dp"), "rep"), check_vma=False
    )
```

```python
import functools

import jax
import jax.numpy as jnp
from jax import lax
from jax.experimental import pallas as pl
from jax.experimental.pallas import tpu as pltpu
from jax.sharding import PartitionSpec as P

damping_frac = 0.01
NB = 128
LANES = 128
SUB = 8
HIGH = lax.Precision.HIGHEST


def iota(shape, dim):
    return lax.broadcasted_iota(jnp.int32, shape, dim)


def dot(a, b, dims, precision=HIGH):
    return lax.dot_general(
        a, b, (dims, ((), ())), precision=precision, preferred_element_type=jnp.float32
    )


def split(x):
    one = x.astype(jnp.bfloat16)
    x = x - one.astype(jnp.float32)
    two = x.astype(jnp.bfloat16)
    three = (x - two.astype(jnp.float32)).astype(jnp.bfloat16)
    return one, two, three


def left_terms(x):
    one, two, three = split(x)
    return jnp.concatenate([one, one, two, two, one, three], axis=1)


def right_terms(x):
    one, two, three = split(x)
    return jnp.concatenate([one, two, one, two, three, one], axis=1)


def by_rows(a, b):
    return dot(a, b, ((1,), (1,)), None)


def project_kernel(steps, rank, place_ref, act_ref, grad_ref, pin_ref, pout_ref, prior_ref, out_ref, pin4, acc, tr):
    step = pl.program_id(0)
    tile = act_ref.shape[2]
    fold = LANES // rank

    @pl.when(step == 0)
    def _():
        for r in range(fold):
            pin4[r * rank : (r + 1) * rank, :] = pin_ref[0]
        acc[...] = jnp.zeros_like(acc)
        tr[...] = jnp.zeros_like(tr)

    in_side = dot(act_ref[0, 0], pin4[...], ((1,), (1,)), None)
    out_side = dot(grad_ref[0, 0], pout_ref[0], ((1,), (1,)), None)
    token = place_ref[0] + step * tile + iota(out_side.shape, 0)
    out_side = jnp.where(token < place_ref[1], out_side, 0.0)
    acc[...] += dot(out_side, in_side, ((0,), (0,)))
    block = prior_ref[0, 0]
    on_diag = iota(block.shape, 0) == iota(block.shape, 1)
    block = jnp.where(on_diag, block, 0.0)
    line = jnp.sum(block, axis=0, keepdims=True)
    tr[0:1, :] += sum(line[:, c : c + LANES] for c in range(0, block.shape[1], LANES))

    @pl.when(step == steps - 1)
    def _():
        rows = rank // fold
        o = iota((rank, LANES), 0)
        lane = iota((rank, LANES), 1)
        kept = jnp.where(lax.rem(o, fold) == lane // rank, acc[...], 0.0)
        pick = (iota((rows, rank), 1) // fold == iota((rows, rank), 0)).astype(jnp.float32)
        vector = dot(pick, kept, ((1,), (0,)))
        for s in range(out_ref.shape[0] - 1):
            out_ref[s] = jnp.where(place_ref[2] == s, vector, 0.0)
        out_ref[out_ref.shape[0] - 1] = tr[...]


def project(place, seqs, activations, out_grads, proj_in, proj_out, fisher_prior):
    steps = 2
    tok, width = activations.shape[2:]
    rank = proj_in.shape[1]
    size = fisher_prior.shape[2]
    tile, blk = tok // steps, size // steps
    rows = size // LANES
    return pl.pallas_call(
        functools.partial(project_kernel, steps, rank),
        grid=(steps,),
        in_specs=[
            pl.BlockSpec(memory_space=pltpu.SMEM),
            pl.BlockSpec((1, 1, tile, width), lambda i: (0, 0, i, 0)),
            pl.BlockSpec((1, 1, tile, width), lambda i: (0, 0, i, 0)),
            pl.BlockSpec((1, rank, width), lambda i: (0, 0, 0)),
            pl.BlockSpec((1, rank, width), lambda i: (0, 0, 0)),
            pl.BlockSpec((1, 1, blk, blk), lambda i: (0, 0, i, i)),
        ],
        out_specs=pl.BlockSpec((seqs + 1, rows, LANES), lambda i: (0, 0, 0)),
        out_shape=jax.ShapeDtypeStruct((seqs + 1, rows, LANES), jnp.float32),
        scratch_shapes=[
            pltpu.VMEM((LANES, width), jnp.bfloat16),
            pltpu.VMEM((rank, LANES), jnp.float32),
            pltpu.VMEM((rows, LANES), jnp.float32),
        ],
        compiler_params=pltpu.CompilerParams(vmem_limit_bytes=60 << 20),
        name="project",
    )(place, activations, out_grads, proj_in, proj_out, fisher_prior)


def reciprocal(p):
    r = pl.reciprocal(p, approx=True)
    return r * (2.0 - p * r)


def spread(x, k):
    return jnp.broadcast_to(x[k : k + 1, :], x.shape)


def lanes_of(x, k):
    return jnp.broadcast_to(x[:, k : k + 1], x.shape)


def solve_group(s, w):
    s = [list(row) for row in s]
    w = list(w)
    pairs = []
    for k in range(0, SUB, 2):
        a, b, c = s[k][k], s[k + 1][k], s[k + 1][k + 1]
        r = reciprocal(a * c - b * b)
        rest = range(k + 2, SUB)
        m = {i: s[i][k] * c - s[i][k + 1] * b for i in rest}
        n = {i: s[i][k + 1] * a - s[i][k] * b for i in rest}
        for i in rest:
            for j in range(k + 2, i + 1):
                s[i][j] = s[i][j] - (m[i] * s[j][k] + n[i] * s[j][k + 1]) * r
        m = {i: m[i] * r for i in rest}
        n = {i: n[i] * r for i in rest}
        for i in rest:
            w[i] = w[i] - (m[i] * w[k] + n[i] * w[k + 1])
        u, v = w[k], w[k + 1]
        w[k], w[k + 1] = (c * u - b * v) * r, (a * v - b * u) * r
        pairs.append((m, n))
    for k in range(SUB - 4, -1, -2):
        m, n = pairs[k // 2]
        for i in range(k + 2, SUB):
            w[k] = w[k] - m[i] * w[i]
            w[k + 1] = w[k + 1] - n[i] * w[i]
    return w


def eliminate(rows):
    groups = len(rows)
    rows = list(rows)
    sub = iota((SUB, LANES), 0)
    lane = iota((SUB, LANES), 1)
    lower, scaled = [], []
    for g in range(groups):
        first = g * SUB
        here = (lane >= first) & (lane < first + SUB)
        unit = (lane - first == sub).astype(jnp.float32)
        own = rows[g]
        cols = [lanes_of(own, first + j) for j in range(SUB)]
        s = [[spread(cols[j], i) for j in range(i + 1)] for i in range(SUB)]
        work = jnp.where(here, unit, own)
        lower.append(jnp.where(lane < first + SUB, work, 0.0))
        picks = solve_group(s, [spread(work, i) for i in range(SUB)])
        work = picks[0]
        for i in range(1, SUB):
            work = jnp.where(sub == i, picks[i], work)
        scaled.append(jnp.where(lane < first + SUB, work, 0.0))
        for h in range(g + 1, groups):
            x = rows[h]
            terms = [lanes_of(x, first + j) * picks[j] for j in range(SUB)]
            while len(terms) > 1:
                terms = [terms[i] + terms[i + 1] for i in range(0, len(terms), 2)]
            rows[h] = jnp.where(here, 0.0, x) - terms[0]
    return lower, scaled


def panel_kernel(c, size, seqs, padded, *refs):
    refs = list(refs)
    tall, wide = 2 * NB, 2 * NB * (c + 1)
    done = wide - tall
    last = wide == size
    place_ref, own_ref, other_ref = refs[:3]
    del refs[:3]
    if c == 0:
        parts_ref = refs.pop(0)
    else:
        aux_ref = refs.pop(0)
        efs, yts, ws, es = (refs[i * c : (i + 1) * c] for i in range(4))
        del refs[: 4 * c]
    if last:
        out_ref, p, ef = refs
    elif c == 0:
        aux_ref, ef_out, yt_out, w_out, e_out, p, ef = refs
    else:
        ef_out, yt_out, w_out, e_out, p, ef = refs

    if c == 0:
        if padded > seqs:
            aux_ref[seqs:padded, :] = jnp.zeros((padded - seqs, size), jnp.float32)
        for b in range(size // LANES):
            aux_ref[0:seqs, b * LANES : (b + 1) * LANES] = parts_ref[0:seqs, b, :]
        v = aux_ref[0:padded, :]
        trace = jnp.sum(parts_ref[seqs]) + jnp.sum(v * v)
        aux_ref[padded:, :] = size / jnp.broadcast_to(trace, (SUB, size))
    scale = aux_ref[padded : padded + 1, :]
    one, two, three = split(aux_ref[0:padded, 0:wide])
    outer_left = jnp.concatenate([x[:, done:] for x in (one, one, two, two, one, three)], axis=0)
    outer_right = jnp.concatenate([one, two, one, two, three, one], axis=0)
    rep = place_ref[0]
    p[pl.ds(rep * NB, NB), :] = own_ref[...]
    p[pl.ds((1 - rep) * NB, NB), :] = other_ref[...]
    outer = dot(outer_left, outer_right, ((0,), (0,)), None)
    eye = iota((tall, wide), 0) + done == iota((tall, wide), 1)
    p[0:tall, :] = (p[0:tall, :] + outer) * scale[:, 0:wide] + jnp.where(eye, damping_frac, 0.0)
    if c:
        p[tall:, 0:done] = ws[c - 1][tall:, :]
    p[tall:, done:] = aux_ref[0:padded, done:wide]

    for k in range(2 * c):
        at, end = k * NB, (k + 1) * NB
        y = by_rows(left_terms(p[0:tall, at:end]), efs[k // 2][k % 2])
        p[0:tall, at:end] = y[:, NB:]
        left = left_terms(p[:, at:end])
        right = right_terms(y[:, :NB])
        if not last:
            yt_out[k] = right
        for b in range(k // 2, c):
            skip = (k + 1 - 2 * b) * NB if k >= 2 * b else 0
            if skip < tall:
                cols = slice(b * tall + skip, (b + 1) * tall)
                p[0:tall, cols] -= by_rows(left[0:tall], yts[b][k, skip:, :])
        p[:, done:] -= by_rows(left, right)
    e_own = []
    for i in range(2):
        at, end = done + i * NB, done + (i + 1) * NB
        low, scl = eliminate([p[i * NB + r : i * NB + r + SUB, at:end] for r in range(0, NB, SUB)])
        for r in range(NB // SUB):
            ef[i, r * SUB : (r + 1) * SUB, :] = low[r]
            ef[i, NB + r * SUB : NB + (r + 1) * SUB, :] = scl[r]
        both = right_terms(ef[i])
        if not last:
            ef_out[i] = both
            e_out[i] = ef[i, 0:NB, :]
        rest = (i + 1) * NB
        y = by_rows(left_terms(p[rest:, at:end]), both)
        p[rest:, at:end] = y[:, NB:]
        if i == 0:
            right = right_terms(y[0:NB, :NB])
            if not last:
                yt_out[2 * c, NB:, :] = right
            p[rest:, end:] -= by_rows(left_terms(y[:, NB:]), right)
    if not last:
        w_out[...] = p[...]
        return
    for k in range(size // NB - 1, -1, -1):
        at, end = k * NB, (k + 1) * NB
        b, row = k // 2, (k % 2) * NB
        e = ef[k % 2, 0:NB, :] if b == c else es[b][k % 2]
        z = dot(p[tall:, at:end], e, ((1,), (0,)))
        p[tall:, at:end] = z
        if k:
            w = (p if b == c else ws[b])[row : row + NB, 0:at]
            p[tall:, 0:at] -= dot(z, w, ((1,), (0,)))
    out_ref[...] = p[tall:, :] * scale


def panel(c, size, seqs, place, own, other, first, state):
    padded = -(-seqs // SUB) * SUB
    tall, wide = 2 * NB, 2 * NB * (c + 1)
    vmem = pl.BlockSpec(memory_space=pltpu.VMEM)
    shape = jax.ShapeDtypeStruct
    if wide == size:
        outs = [shape((padded, size), jnp.float32)]
    else:
        outs = [
            shape((2, 2 * NB, 6 * NB), jnp.bfloat16),
            shape((2 * c + 1, tall, 6 * NB), jnp.bfloat16),
            shape((tall + padded, wide), jnp.float32),
            shape((2, NB, NB), jnp.float32),
        ]
        if c == 0:
            outs = [shape((padded + SUB, size), jnp.float32)] + outs
    earlier = [x for kind in zip(*state) for x in kind] if state else []
    return pl.pallas_call(
        functools.partial(panel_kernel, c, size, seqs, padded),
        in_specs=[pl.BlockSpec(memory_space=pltpu.SMEM)] + [vmem] * (3 + len(earlier)),
        out_specs=[vmem] * len(outs),
        out_shape=outs,
        scratch_shapes=[
            pltpu.VMEM((tall + padded, wide), jnp.float32),
            pltpu.VMEM((2, 2 * NB, NB), jnp.float32),
        ],
        compiler_params=pltpu.CompilerParams(vmem_limit_bytes=40 << 20),
        cost_estimate=pl.CostEstimate(flops=12_000_000_000, bytes_accessed=4_000_000, transcendentals=0),
        name="panel%d" % c,
    )(place, own, other, first, *earlier)


def score_kernel(solved_ref, query_ref, out_ref):
    rows = solved_ref.shape[0]
    terms = by_rows(jnp.concatenate(split(solved_ref[...]), axis=0), query_ref[...])
    out_ref[...] = terms[0:rows] + terms[rows : 2 * rows] + terms[2 * rows :]


def score(solved, queries):
    vmem = pl.BlockSpec(memory_space=pltpu.VMEM)
    return pl.pallas_call(
        score_kernel,
        in_specs=[vmem, vmem],
        out_specs=vmem,
        out_shape=jax.ShapeDtypeStruct((solved.shape[0], queries.shape[0]), jnp.float32),
        name="score",
    )(solved, queries)


def sum_to_middle(x):
    n = lax.axis_size("dp")
    for s in range(n // 2 - 1):
        x = x + lax.ppermute(x, "dp", [(s, s + 1), (n - 1 - s, n - 2 - s)])
    if n > 1:
        m = n // 2
        x = x + lax.ppermute(x, "dp", [(m - 1, m), (m, m - 1)])
    return x


def from_middle(x):
    n = lax.axis_size("dp")
    here = lax.axis_index("dp")
    for s in range(n // 2 - 2, -1, -1):
        got = lax.ppermute(x, "dp", [(s + 1, s), (n - 2 - s, n - 1 - s)])
        x = jnp.where((here == s) | (here == n - 1 - s), got, x)
    return x


SWAP = [(0, 1), (1, 0)]


def after(x, *others):
    return lax.optimization_barrier((x,) + others)[0]


def body(activations, out_grads, proj_in, proj_out, seq_lengths, fisher_prior, query_grads):
    tok_half = activations.shape[2]
    prior = fisher_prior[0, 0]
    size = prior.shape[0]
    seqs = lax.axis_size("dp")
    rep, dp = lax.axis_index("rep"), lax.axis_index("dp")
    count = size // (2 * NB)

    def over_rep(c, array):
        top, wide = 2 * c * NB, 2 * (c + 1) * NB
        other = lax.dynamic_slice(array, (top + (1 - rep) * NB, 0), (NB, wide))
        own = lax.dynamic_slice(array, (top + rep * NB, 0), (NB, wide))
        return own + lax.ppermute(other, "rep", SWAP)

    sums = [over_rep(0, prior)]
    place = jnp.stack([rep * tok_half, seq_lengths[0], dp]).astype(jnp.int32)
    part = project(after(place, sums[0]), seqs, activations, out_grads, proj_in, proj_out, fisher_prior)
    prior = after(prior, part)
    sums += [over_rep(c, prior) for c in range(1, count)]
    part = sum_to_middle(part + lax.ppermute(part, "rep", SWAP))
    sums = [sum_to_middle(x) for x in sums]
    queries = lax.all_gather(after(query_grads[0, 0], sums[-1]), "dp", axis=0, tiled=True)
    place = rep.astype(jnp.int32).reshape(1)
    state, first = [], part
    for c in range(count):
        out = panel(c, size, seqs, place, sums[c], lax.ppermute(sums[c], "rep", SWAP), first, state)
        if c == 0:
            first, out = out[0], out[1:]
        state.append(out)
    scores = from_middle(score(out[0], queries))
    return lax.psum(lax.dynamic_slice(scores, (dp, 0), (1, scores.shape[1])), "mod")


def solution(mesh):
    placed = (
        P("mod", ("grp", "dp"), "rep", None),
        P("mod", ("grp", "dp"), "rep", None),
        P("mod", None, None),
        P("mod", None, None),
        P(("grp", "dp")),
        P("mod", ("grp", "dp", "rep"), None, None),
        P("mod", "rep", "dp", None),
    )
    return jax.shard_map(
        body, mesh=mesh, in_specs=placed, out_specs=P(("grp", "dp"), "rep"), check_vma=False
    )
```

```python
import functools

import jax
import jax.numpy as jnp
from jax import lax
from jax.experimental import pallas as pl
from jax.experimental.pallas import tpu as pltpu
from jax.sharding import PartitionSpec as P

damping_frac = 0.01
NB = 128
LANES = 128
SUB = 8
HIGH = lax.Precision.HIGHEST


def iota(shape, dim):
    return lax.broadcasted_iota(jnp.int32, shape, dim)


def dot(a, b, dims, precision=HIGH):
    return lax.dot_general(
        a, b, (dims, ((), ())), precision=precision, preferred_element_type=jnp.float32
    )


def split(x):
    one = x.astype(jnp.bfloat16)
    x = x - one.astype(jnp.float32)
    two = x.astype(jnp.bfloat16)
    three = (x - two.astype(jnp.float32)).astype(jnp.bfloat16)
    return one, two, three


def left_terms(x):
    one, two, three = split(x)
    return jnp.concatenate([one, one, two, two, one, three], axis=1)


def right_terms(x):
    one, two, three = split(x)
    return jnp.concatenate([one, two, one, two, three, one], axis=1)


def by_rows(a, b):
    return dot(a, b, ((1,), (1,)), None)


def project_kernel(steps, rank, seqs, place_ref, act_ref, grad_ref, pin_ref, pout_ref, prior_ref, out_ref, pin4, acc, tr):
    step = pl.program_id(0)
    tile = act_ref.shape[2]
    fold = LANES // rank

    @pl.when(step == 0)
    def _():
        for r in range(fold):
            pin4[r * rank : (r + 1) * rank, :] = pin_ref[0]
        acc[...] = jnp.zeros_like(acc)
        tr[...] = jnp.zeros_like(tr)
        head = out_ref.shape[0] - 3 * NB
        for i, (row, col) in enumerate(((0, 0), (NB, 0), (NB, NB))):
            out_ref[head + i * NB : head + (i + 1) * NB, :] = prior_ref[0, 0, row : row + NB, col : col + NB]

    in_side = dot(act_ref[0, 0], pin4[...], ((1,), (1,)), None)
    out_side = dot(grad_ref[0, 0], pout_ref[0], ((1,), (1,)), None)
    token = place_ref[0] + step * tile + iota(out_side.shape, 0)
    out_side = jnp.where(token < place_ref[1], out_side, 0.0)
    acc[...] += dot(out_side, in_side, ((0,), (0,)))
    block = prior_ref[0, 0]
    on_diag = iota(block.shape, 0) == iota(block.shape, 1)
    block = jnp.where(on_diag, block, 0.0)
    line = jnp.sum(block, axis=0, keepdims=True)
    tr[0:1, :] += sum(line[:, c : c + LANES] for c in range(0, block.shape[1], LANES))

    @pl.when(step == steps - 1)
    def _():
        rows = rank // fold
        o = iota((rank, LANES), 0)
        lane = iota((rank, LANES), 1)
        kept = jnp.where(lax.rem(o, fold) == lane // rank, acc[...], 0.0)
        pick = (iota((rows, rank), 1) // fold == iota((rows, rank), 0)).astype(jnp.float32)
        vector = dot(pick, kept, ((1,), (0,)))
        for s in range(seqs):
            out_ref[s * rows : (s + 1) * rows, :] = jnp.where(place_ref[2] == s, vector, 0.0)
        out_ref[seqs * rows : (seqs + 1) * rows, :] = tr[...]


def project(place, seqs, activations, out_grads, proj_in, proj_out, fisher_prior):
    steps = 2
    tok, width = activations.shape[2:]
    rank = proj_in.shape[1]
    size = fisher_prior.shape[2]
    tile, blk = tok // steps, size // steps
    rows = size // LANES
    height = (seqs + 1) * rows + 3 * NB
    return pl.pallas_call(
        functools.partial(project_kernel, steps, rank, seqs),
        grid=(steps,),
        in_specs=[
            pl.BlockSpec(memory_space=pltpu.SMEM),
            pl.BlockSpec((1, 1, tile, width), lambda i: (0, 0, i, 0)),
            pl.BlockSpec((1, 1, tile, width), lambda i: (0, 0, i, 0)),
            pl.BlockSpec((1, rank, width), lambda i: (0, 0, 0)),
            pl.BlockSpec((1, rank, width), lambda i: (0, 0, 0)),
            pl.BlockSpec((1, 1, blk, blk), lambda i: (0, 0, i, i)),
        ],
        out_specs=pl.BlockSpec((height, LANES), lambda i: (0, 0)),
        out_shape=jax.ShapeDtypeStruct((height, LANES), jnp.float32),
        scratch_shapes=[
            pltpu.VMEM((LANES, width), jnp.bfloat16),
            pltpu.VMEM((rank, LANES), jnp.float32),
            pltpu.VMEM((rows, LANES), jnp.float32),
        ],
        compiler_params=pltpu.CompilerParams(vmem_limit_bytes=60 << 20),
        name="project",
    )(place, activations, out_grads, proj_in, proj_out, fisher_prior)


def reciprocal(p):
    return pl.reciprocal(p, approx=True)


def spread(x, k):
    return jnp.broadcast_to(x[k : k + 1, :], x.shape)


def lanes_of(x, k):
    return jnp.broadcast_to(x[:, k : k + 1], x.shape)


def solve_group(s, w):
    s = [list(row) for row in s]
    w = list(w)
    pairs = []
    for k in range(0, SUB, 2):
        a, b, c = s[k][k], s[k + 1][k], s[k + 1][k + 1]
        r = reciprocal(a * c - b * b)
        rest = range(k + 2, SUB)
        m = {i: s[i][k] * c - s[i][k + 1] * b for i in rest}
        n = {i: s[i][k + 1] * a - s[i][k] * b for i in rest}
        for i in rest:
            for j in range(k + 2, i + 1):
                s[i][j] = s[i][j] - (m[i] * s[j][k] + n[i] * s[j][k + 1]) * r
        m = {i: m[i] * r for i in rest}
        n = {i: n[i] * r for i in rest}
        for i in rest:
            w[i] = w[i] - (m[i] * w[k] + n[i] * w[k + 1])
        u, v = w[k], w[k + 1]
        w[k], w[k + 1] = (c * u - b * v) * r, (a * v - b * u) * r
        pairs.append((m, n))
    for k in range(SUB - 4, -1, -2):
        m, n = pairs[k // 2]
        for i in range(SUB - 2, k, -2):
            w[k] = w[k] - (m[i] * w[i] + m[i + 1] * w[i + 1])
            w[k + 1] = w[k + 1] - (n[i] * w[i] + n[i + 1] * w[i + 1])
    return w


def eliminate(rows):
    groups = len(rows)
    rows = list(rows)
    sub = iota((SUB, LANES), 0)
    lane = iota((SUB, LANES), 1)
    lower, scaled = [], []
    for g in range(groups):
        first = g * SUB
        here = (lane >= first) & (lane < first + SUB)
        unit = (lane - first == sub).astype(jnp.float32)
        own = rows[g]
        cols = [lanes_of(own, first + j) for j in range(SUB)]
        s = [[spread(cols[j], i) for j in range(i + 1)] for i in range(SUB)]
        work = jnp.where(here, unit, own)
        lower.append(jnp.where(lane < first + SUB, work, 0.0))
        picks = solve_group(s, [spread(work, i) for i in range(SUB)])
        work = picks[0]
        for i in range(1, SUB):
            work = jnp.where(sub == i, picks[i], work)
        scaled.append(jnp.where(lane < first + SUB, work, 0.0))
        for h in range(g + 1, groups):
            x = rows[h]
            terms = [lanes_of(x, first + j) * picks[j] for j in range(SUB)]
            while len(terms) > 1:
                terms = [terms[i] + terms[i + 1] for i in range(0, len(terms), 2)]
            rows[h] = jnp.where(here, 0.0, x) - terms[0]
    return lower, scaled


def panel_kernel(c, size, seqs, padded, *refs):
    refs = list(refs)
    tall, wide = 2 * NB, 2 * NB * (c + 1)
    done = wide - tall
    last = wide == size
    if c == 0:
        first_ref = refs.pop(0)
        head = first_ref.shape[0] - 3 * NB
        rows = size // LANES
    else:
        place_ref, own_ref, other_ref, aux_ref = refs[:4]
        del refs[:4]
        efs, yts, ws, es = (refs[i * c : (i + 1) * c] for i in range(4))
        del refs[: 4 * c]
    if last:
        out_ref, p, ef = refs
    elif c == 0:
        aux_ref, ef_out, yt_out, w_out, e_out, p, ef = refs
    else:
        ef_out, yt_out, w_out, e_out, p, ef = refs

    if c == 0:
        if padded > seqs:
            aux_ref[seqs:padded, :] = jnp.zeros((padded - seqs, size), jnp.float32)
        for r in range(seqs * rows):
            at = r % rows * LANES
            aux_ref[r // rows : r // rows + 1, at : at + LANES] = first_ref[r : r + 1, :]
        v = aux_ref[0:padded, :]
        trace = jnp.sum(first_ref[seqs * rows : head, :]) + jnp.sum(v * v)
        aux_ref[padded:, :] = size / jnp.broadcast_to(trace, (SUB, size))
    scale = aux_ref[padded : padded + 1, :]
    one, two, three = split(aux_ref[0:padded, 0:wide])
    outer_left = jnp.concatenate([x[:, done:] for x in (one, one, two, two, one, three)], axis=0)
    outer_right = jnp.concatenate([one, two, one, two, three, one], axis=0)
    if c == 0:
        p[0:NB, 0:NB] = first_ref[head : head + NB, :]
        p[0:NB, NB:] = jnp.zeros((NB, NB), jnp.float32)
        p[NB:tall, 0:NB] = first_ref[head + NB : head + 2 * NB, :]
        p[NB:tall, NB:] = first_ref[head + 2 * NB :, :]
    else:
        rep = place_ref[0]
        p[pl.ds(rep * NB, NB), :] = own_ref[...]
        p[pl.ds((1 - rep) * NB, NB), :] = other_ref[...]
    outer = dot(outer_left, outer_right, ((0,), (0,)), None)
    eye = iota((tall, wide), 0) + done == iota((tall, wide), 1)
    p[0:tall, :] = (p[0:tall, :] + outer) * scale[:, 0:wide] + jnp.where(eye, damping_frac, 0.0)
    if c:
        p[tall:, 0:done] = ws[c - 1][tall:, :]
    p[tall:, done:] = aux_ref[0:padded, done:wide]

    for k in range(2 * c):
        at, end = k * NB, (k + 1) * NB
        y = by_rows(left_terms(p[0:tall, at:end]), efs[k // 2][k % 2])
        p[0:tall, at:end] = y[:, NB:]
        left = left_terms(p[:, at:end])
        right = right_terms(y[:, :NB])
        if not last:
            yt_out[k] = right
        for b in range(k // 2, c):
            skip = (k + 1 - 2 * b) * NB if k >= 2 * b else 0
            if skip < tall:
                cols = slice(b * tall + skip, (b + 1) * tall)
                p[0:tall, cols] -= by_rows(left[0:tall], yts[b][k, skip:, :])
        p[:, done:] -= by_rows(left, right)
    e_own = []
    for i in range(2):
        at, end = done + i * NB, done + (i + 1) * NB
        low, scl = eliminate([p[i * NB + r : i * NB + r + SUB, at:end] for r in range(0, NB, SUB)])
        for r in range(NB // SUB):
            ef[i, r * SUB : (r + 1) * SUB, :] = low[r]
            ef[i, NB + r * SUB : NB + (r + 1) * SUB, :] = scl[r]
        both = right_terms(ef[i])
        if not last:
            ef_out[i] = both
            e_out[i] = ef[i, 0:NB, :]
        rest = (i + 1) * NB
        y = by_rows(left_terms(p[rest:, at:end]), both)
        p[rest:, at:end] = y[:, NB:]
        if i == 0:
            right = right_terms(y[0:NB, :NB])
            if not last:
                yt_out[2 * c, NB:, :] = right
            p[rest:, end:] -= by_rows(left_terms(y[:, NB:]), right)
    if not last:
        w_out[...] = p[...]
        return
    for k in range(size // NB - 1, -1, -1):
        at, end = k * NB, (k + 1) * NB
        b, row = k // 2, (k % 2) * NB
        e = ef[k % 2, 0:NB, :] if b == c else es[b][k % 2]
        z = dot(p[tall:, at:end], e, ((1,), (0,)))
        p[tall:, at:end] = z
        if k:
            w = (p if b == c else ws[b])[row : row + NB, 0:at]
            p[tall:, 0:at] -= dot(z, w, ((1,), (0,)))
    out_ref[...] = p[tall:, :] * scale


def panel(c, size, seqs, inputs, state):
    padded = -(-seqs // SUB) * SUB
    tall, wide = 2 * NB, 2 * NB * (c + 1)
    vmem = pl.BlockSpec(memory_space=pltpu.VMEM)
    shape = jax.ShapeDtypeStruct
    if wide == size:
        outs = [shape((padded, size), jnp.float32)]
    else:
        outs = [
            shape((2, 2 * NB, 6 * NB), jnp.bfloat16),
            shape((2 * c + 1, tall, 6 * NB), jnp.bfloat16),
            shape((tall + padded, wide), jnp.float32),
            shape((2, NB, NB), jnp.float32),
        ]
        if c == 0:
            outs = [shape((padded + SUB, size), jnp.float32)] + outs
    earlier = [x for kind in zip(*state) for x in kind] if state else []
    return pl.pallas_call(
        functools.partial(panel_kernel, c, size, seqs, padded),
        in_specs=([pl.BlockSpec(memory_space=pltpu.SMEM)] + [vmem] * 3 if c else [vmem]) + [vmem] * len(earlier),
        out_specs=[vmem] * len(outs),
        out_shape=outs,
        scratch_shapes=[
            pltpu.VMEM((tall + padded, wide), jnp.float32),
            pltpu.VMEM((2, 2 * NB, NB), jnp.float32),
        ],
        compiler_params=pltpu.CompilerParams(vmem_limit_bytes=24 << 20),
        cost_estimate=pl.CostEstimate(flops=12_000_000_000, bytes_accessed=4_000_000, transcendentals=0),
        name="panel%d" % c,
    )(*inputs, *earlier)


def score_kernel(solved_ref, query_ref, out_ref):
    rows = solved_ref.shape[0]
    terms = by_rows(jnp.concatenate(split(solved_ref[...]), axis=0), query_ref[...])
    out_ref[...] = terms[0:rows] + terms[rows : 2 * rows] + terms[2 * rows :]


def score(solved, queries):
    vmem = pl.BlockSpec(memory_space=pltpu.VMEM)
    return pl.pallas_call(
        score_kernel,
        in_specs=[vmem, vmem],
        out_specs=vmem,
        out_shape=jax.ShapeDtypeStruct((solved.shape[0], queries.shape[0]), jnp.float32),
        name="score",
    )(solved, queries)


def after(x, *others):
    return lax.optimization_barrier((x,) + others)[0]


def inward(n):
    steps = [[(s, s + 1), (n - 1 - s, n - 2 - s)] for s in range(n // 2 - 1)]
    return steps + [[(n // 2 - 1, n // 2), (n // 2, n // 2 - 1)]] if n > 1 else []


def from_middle(x):
    n = lax.axis_size("dp")
    here = lax.axis_index("dp")
    for s in range(n // 2 - 2, -1, -1):
        got = lax.ppermute(x, "dp", [(s + 1, s), (n - 2 - s, n - 1 - s)])
        x = jnp.where((here == s) | (here == n - 1 - s), got, x)
    return x


SWAP = [(0, 1), (1, 0)]


def body(activations, out_grads, proj_in, proj_out, seq_lengths, fisher_prior, query_grads):
    tok_half = activations.shape[2]
    prior = fisher_prior[0, 0]
    size = prior.shape[0]
    seqs = lax.axis_size("dp")
    rep, dp = lax.axis_index("rep"), lax.axis_index("dp")
    count = size // (2 * NB)
    steps = inward(seqs)

    def over_rep(c, gate):
        top, wide = 2 * c * NB, 2 * (c + 1) * NB
        array = prior if gate is None else after(prior, gate)
        other = lax.dynamic_slice(array, (top + (1 - rep) * NB, 0), (NB, wide))
        own = lax.dynamic_slice(array, (top + rep * NB, 0), (NB, wide))
        return own, lax.ppermute(other, "rep", SWAP)

    second = over_rep(1, None)
    place = jnp.stack([rep * tok_half, seq_lengths[0], dp]).astype(jnp.int32)
    first = project(place, seqs, activations, out_grads, proj_in, proj_out, fisher_prior)
    first = first + lax.ppermute(first, "rep", SWAP)
    came = first
    for i, step in enumerate(steps):
        first = first + lax.ppermute(first, "dp", step)
        if i == 0:
            came = first
    sums = [None, after(second[0], came) + second[1]]
    sums += [sum(over_rep(c, came)) for c in range(2, count)]
    queries = lax.all_gather(after(query_grads[0, 0], first), "dp", axis=0, tiled=True)
    out = panel(0, size, seqs, [first], [])
    aux, state = out[0], [out[1:]]
    place = rep.astype(jnp.int32).reshape(1)
    done = [aux]
    for c in range(1, count):
        x = sums[c]
        for i, step in enumerate(steps):
            got = lax.ppermute(x, "dp", step)
            if i == len(steps) - 1:
                got = after(got, done[c - 1])
            elif c > 1:
                got = after(got, done[c - 2])
            x = x + got
        out = panel(c, size, seqs, [place, x, lax.ppermute(x, "rep", SWAP), aux], state)
        state.append(out)
        done.append(out[0])
    scores = from_middle(score(out[0], queries))
    mine = lax.dynamic_slice(scores, (dp, 0), (1, scores.shape[1]))
    if lax.axis_size("mod") == 2:
        return mine + lax.ppermute(mine, "mod", SWAP)
    return lax.psum(mine, "mod")


def solution(mesh):
    placed = (
        P("mod", ("grp", "dp"), "rep", None),
        P("mod", ("grp", "dp"), "rep", None),
        P("mod", None, None),
        P("mod", None, None),
        P(("grp", "dp")),
        P("mod", ("grp", "dp", "rep"), None, None),
        P("mod", "rep", "dp", None),
    )
    return jax.shard_map(
        body, mesh=mesh, in_specs=placed, out_specs=P(("grp", "dp"), "rep"), check_vma=False
    )
```

```python
import functools

import jax
import jax.numpy as jnp
from jax import lax
from jax.experimental import pallas as pl
from jax.experimental.pallas import tpu as pltpu
from jax.sharding import PartitionSpec as P

damping_frac = 0.01
NB = 128
LANES = 128
SUB = 8
HIGH = lax.Precision.HIGHEST


def iota(shape, dim):
    return lax.broadcasted_iota(jnp.int32, shape, dim)


def dot(a, b, dims, precision=HIGH):
    return lax.dot_general(
        a, b, (dims, ((), ())), precision=precision, preferred_element_type=jnp.float32
    )


def split(x):
    one = x.astype(jnp.bfloat16)
    x = x - one.astype(jnp.float32)
    two = x.astype(jnp.bfloat16)
    three = (x - two.astype(jnp.float32)).astype(jnp.bfloat16)
    return one, two, three


def left_terms(x):
    one, two, three = split(x)
    return jnp.concatenate([one, one, two, two, one, three], axis=1)


def right_terms(x):
    one, two, three = split(x)
    return jnp.concatenate([one, two, one, two, three, one], axis=1)


def three_terms(x):
    return jnp.concatenate(split(x), axis=1)


def right_six(x):
    one, two, three = x[:, :NB], x[:, NB : 2 * NB], x[:, 2 * NB :]
    return jnp.concatenate([one, two, one, two, three, one], axis=1)


def by_rows(a, b):
    return dot(a, b, ((1,), (1,)), None)


def project_kernel(steps, seqs, place_ref, act_ref, grad_ref, pin_ref, pout_ref, prior_ref, out_ref, ins, outs, tr):
    step = pl.program_id(0)
    in_side = by_rows(act_ref[0, 0], pin_ref[0])
    out_side = by_rows(grad_ref[0, 0], pout_ref[0])
    block = prior_ref[0, 0]
    on_diag = iota(block.shape, 0) == iota(block.shape, 1)
    line = jnp.sum(jnp.where(on_diag, block, 0.0), axis=0, keepdims=True)
    line = sum(line[:, c : c + LANES] for c in range(0, block.shape[1], LANES))

    @pl.when(step == 0)
    def _():
        ins[...] = in_side
        outs[...] = out_side
        tr[...] = jnp.zeros_like(tr)
        tr[0:1, :] = line
        head = out_ref.shape[0] - 3 * NB
        for i, (row, col) in enumerate(((0, 0), (NB, 0), (NB, NB))):
            out_ref[head + i * NB : head + (i + 1) * NB, :] = block[row : row + NB, col : col + NB]

    @pl.when(step > 0)
    def _():
        ins[...] += in_side
        outs[...] += out_side
        tr[0:1, :] += line

    @pl.when(step == steps - 1)
    def _():
        rank = ins.shape[1]
        fold = LANES // rank
        rows = rank // fold
        token = place_ref[0] + iota(outs.shape, 0)
        kept = jnp.where(token < place_ref[1], outs[...], 0.0)
        matrix = dot(kept, ins[...], ((0,), (0,)))
        copies = (iota((rank, LANES), 0) == lax.rem(iota((rank, LANES), 1), rank)).astype(jnp.float32)
        matrix = dot(matrix, copies, ((1,), (0,)))
        o = iota((rank, LANES), 0)
        lane = iota((rank, LANES), 1)
        matrix = jnp.where(lax.rem(o, fold) == lane // rank, matrix, 0.0)
        pick = (iota((rows, rank), 1) // fold == iota((rows, rank), 0)).astype(jnp.float32)
        vector = dot(pick, matrix, ((1,), (0,)))
        for s in range(seqs):
            out_ref[s * rows : (s + 1) * rows, :] = jnp.where(place_ref[2] == s, vector, 0.0)
        out_ref[seqs * rows : (seqs + 1) * rows, :] = tr[...]


def project(place, seqs, activations, out_grads, proj_in, proj_out, fisher_prior):
    steps = 4
    tok, width = activations.shape[2:]
    rank = proj_in.shape[1]
    size = fisher_prior.shape[2]
    part, blk = width // steps, size // steps
    rows = size // LANES
    height = (seqs + 1) * rows + 3 * NB
    return pl.pallas_call(
        functools.partial(project_kernel, steps, seqs),
        grid=(steps,),
        in_specs=[
            pl.BlockSpec(memory_space=pltpu.SMEM),
            pl.BlockSpec((1, 1, tok, part), lambda i: (0, 0, 0, i)),
            pl.BlockSpec((1, 1, tok, part), lambda i: (0, 0, 0, i)),
            pl.BlockSpec((1, rank, part), lambda i: (0, 0, i)),
            pl.BlockSpec((1, rank, part), lambda i: (0, 0, i)),
            pl.BlockSpec((1, 1, blk, blk), lambda i: (0, 0, i, i)),
        ],
        out_specs=pl.BlockSpec((height, LANES), lambda i: (0, 0)),
        out_shape=jax.ShapeDtypeStruct((height, LANES), jnp.float32),
        scratch_shapes=[
            pltpu.VMEM((tok, rank), jnp.float32),
            pltpu.VMEM((tok, rank), jnp.float32),
            pltpu.VMEM((rows, LANES), jnp.float32),
        ],
        compiler_params=pltpu.CompilerParams(vmem_limit_bytes=60 << 20),
        name="project",
    )(place, activations, out_grads, proj_in, proj_out, fisher_prior)


def reciprocal(p):
    return pl.reciprocal(p, approx=True)


def spread(x, k):
    return jnp.broadcast_to(x[k : k + 1, :], x.shape)


def lanes_of(x, k):
    return jnp.broadcast_to(x[:, k : k + 1], x.shape)


def solve_group(s, w):
    s = [list(row) for row in s]
    w = list(w)
    pairs = []
    for k in range(0, SUB, 2):
        a, b, c = s[k][k], s[k + 1][k], s[k + 1][k + 1]
        r = reciprocal(a * c - b * b)
        rest = range(k + 2, SUB)
        m = {i: s[i][k] * c - s[i][k + 1] * b for i in rest}
        n = {i: s[i][k + 1] * a - s[i][k] * b for i in rest}
        for i in rest:
            for j in range(k + 2, i + 1):
                s[i][j] = s[i][j] - (m[i] * s[j][k] + n[i] * s[j][k + 1]) * r
        m = {i: m[i] * r for i in rest}
        n = {i: n[i] * r for i in rest}
        for i in rest:
            w[i] = w[i] - (m[i] * w[k] + n[i] * w[k + 1])
        u, v = w[k], w[k + 1]
        w[k], w[k + 1] = (c * u - b * v) * r, (a * v - b * u) * r
        pairs.append((m, n))
    for k in range(SUB - 4, -1, -2):
        m, n = pairs[k // 2]
        for i in range(SUB - 2, k, -2):
            w[k] = w[k] - (m[i] * w[i] + m[i + 1] * w[i + 1])
            w[k + 1] = w[k + 1] - (n[i] * w[i] + n[i + 1] * w[i + 1])
    return w


def eliminate(rows):
    groups = len(rows)
    rows = list(rows)
    sub = iota((SUB, LANES), 0)
    lane = iota((SUB, LANES), 1)
    lower, scaled = [], []
    for g in range(groups):
        first = g * SUB
        here = (lane >= first) & (lane < first + SUB)
        unit = (lane - first == sub).astype(jnp.float32)
        own = rows[g]
        cols = [lanes_of(own, first + j) for j in range(SUB)]
        s = [[spread(cols[j], i) for j in range(i + 1)] for i in range(SUB)]
        work = jnp.where(here, unit, own)
        lower.append(jnp.where(lane < first + SUB, work, 0.0))
        picks = solve_group(s, [spread(work, i) for i in range(SUB)])
        work = picks[0]
        for i in range(1, SUB):
            work = jnp.where(sub == i, picks[i], work)
        scaled.append(jnp.where(lane < first + SUB, work, 0.0))
        for h in range(g + 1, groups):
            x = rows[h]
            terms = [lanes_of(x, first + j) * picks[j] for j in range(SUB)]
            while len(terms) > 1:
                terms = [terms[i] + terms[i + 1] for i in range(0, len(terms), 2)]
            rows[h] = jnp.where(here, 0.0, x) - terms[0]
    return lower, scaled


def panel_kernel(c, size, seqs, padded, *refs):
    refs = list(refs)
    tall, wide = 2 * NB, 2 * NB * (c + 1)
    done = wide - tall
    last = wide == size
    waits = {}

    def start(name, source, target, sem):
        waits[name] = pltpu.make_async_copy(source, target, sem)
        waits[name].start()

    def wait(name):
        if name in waits:
            waits.pop(name).wait()

    if c == 0:
        first_ref = refs.pop(0)
        head = first_ref.shape[0] - 3 * NB
        rows = size // LANES
    else:
        place_ref, half_ref, got_ref, half_other_ref, got_other_ref, aux_ref, x_ref = refs[:7]
        del refs[:7]
    kept = c + (c if last else 0)
    given = refs[:kept]
    del refs[:kept]
    if last:
        out_ref = refs.pop(0)
    else:
        if c == 0:
            aux_ref = refs.pop(0)
        x_out, terms_out, w_out = refs[:3]
        del refs[:3]
    p, ef, terms, sems = refs[:4]
    held = refs[4:]
    for b in range(kept):
        start(("terms", b) if b < c else ("w", b - c), given[b], held[b], sems.at[b])

    if c == 0:
        if padded > seqs:
            aux_ref[seqs:padded, :] = jnp.zeros((padded - seqs, size), jnp.float32)
        for r in range(seqs * rows):
            at = r % rows * LANES
            aux_ref[r // rows : r // rows + 1, at : at + LANES] = first_ref[r : r + 1, :]
        v = aux_ref[0:padded, :]
        trace = jnp.sum(first_ref[seqs * rows : head, :]) + jnp.sum(v * v)
        aux_ref[padded:, :] = size / jnp.broadcast_to(trace, (SUB, size))
    scale = aux_ref[padded : padded + 1, :]
    one, two, three = split(aux_ref[0:padded, 0:wide])
    outer_left = jnp.concatenate([x[:, done:] for x in (one, one, two, two, one, three)], axis=0)
    outer_right = jnp.concatenate([one, two, one, two, three, one], axis=0)
    if c == 0:
        p[0:NB, 0:NB] = first_ref[head : head + NB, :]
        p[0:NB, NB:] = jnp.zeros((NB, NB), jnp.float32)
        p[NB:tall, 0:NB] = first_ref[head + NB : head + 2 * NB, :]
        p[NB:tall, NB:] = first_ref[head + 2 * NB :, :]
    else:
        rep = place_ref[0]
        p[pl.ds(rep * NB, NB), :] = half_ref[...] + got_ref[...]
        p[pl.ds((1 - rep) * NB, NB), :] = half_other_ref[...] + got_other_ref[...]
    outer = dot(outer_left, outer_right, ((0,), (0,)), None)
    eye = iota((tall, wide), 0) + done == iota((tall, wide), 1)
    p[0:tall, :] = (p[0:tall, :] + outer) * scale[:, 0:wide] + jnp.where(eye, damping_frac, 0.0)
    if c:
        p[tall:, 0:done] = x_ref[...]
    p[tall:, done:] = aux_ref[0:padded, done:wide]

    for k in range(2 * c):
        at, end = k * NB, (k + 1) * NB
        wait(("terms", k // 2))
        both = right_six(held[k // 2][k % 2 * tall : (k % 2 + 1) * tall, :])
        y = by_rows(left_terms(p[0:tall, at:end]), both)
        p[0:tall, at:end] = y[:, NB:]
        left = left_terms(p[:, at:end])
        if not last:
            terms[(2 + k) * tall : (3 + k) * tall, :] = three_terms(y[:, :NB])
        for b in range(k // 2, c):
            skip = (k + 1 - 2 * b) * NB if k >= 2 * b else 0
            if skip < tall:
                wait(("terms", b))
                cols = slice(b * tall + skip, (b + 1) * tall)
                right = right_six(held[b][(2 + k) * tall + skip : (3 + k) * tall, :])
                p[0:tall, cols] -= by_rows(left[0:tall], right)
        p[:, done:] -= by_rows(left, right_terms(y[:, :NB]))
    for i in range(2):
        at, end = done + i * NB, done + (i + 1) * NB
        low, scl = eliminate([p[i * NB + r : i * NB + r + SUB, at:end] for r in range(0, NB, SUB)])
        for r in range(NB // SUB):
            ef[i, r * SUB : (r + 1) * SUB, :] = low[r]
            ef[i, NB + r * SUB : NB + (r + 1) * SUB, :] = scl[r]
        if not last:
            terms[i * tall : (i + 1) * tall, :] = three_terms(ef[i])
        both = right_terms(ef[i])
        rest = (i + 1) * NB
        y = by_rows(left_terms(p[rest:, at:end]), both)
        p[rest:, at:end] = y[:, NB:]
        if i == 0:
            if not last:
                terms[(2 + 2 * c) * tall : (2 + 2 * c) * tall + NB, :] = jnp.zeros((NB, 3 * NB), jnp.bfloat16)
                terms[(2 + 2 * c) * tall + NB :, :] = three_terms(y[0:NB, :NB])
            p[rest:, end:] -= by_rows(left_terms(y[:, NB:]), right_terms(y[0:NB, :NB]))
    if not last:
        x_out[...] = p[tall:, :]
        start("terms", terms, terms_out, sems.at[kept])
        start("w", p.at[0:tall, :], w_out, sems.at[kept + 1])
        wait("terms")
        wait("w")
        return
    for k in range(size // NB - 1, -1, -1):
        at, end = k * NB, (k + 1) * NB
        b, row = k // 2, (k % 2) * NB
        if b == c:
            e, w = ef[k % 2, 0:NB, :], p[row : row + NB, 0:at]
        else:
            e = held[b][k % 2 * tall : k % 2 * tall + NB, :].astype(jnp.float32)
            e = e[:, :NB] + e[:, NB : 2 * NB] + e[:, 2 * NB :]
            wait(("w", b))
            w = held[c + b][row : row + NB, 0:at]
        z = dot(p[tall:, at:end], e, ((1,), (0,)))
        p[tall:, at:end] = z
        if k:
            p[tall:, 0:at] -= dot(z, w, ((1,), (0,)))
    out_ref[...] = p[tall:, :] * scale


def panel(c, size, seqs, inputs, state):
    padded = -(-seqs // SUB) * SUB
    tall, wide = 2 * NB, 2 * NB * (c + 1)
    last = wide == size
    vmem, hbm = pl.BlockSpec(memory_space=pltpu.VMEM), pl.BlockSpec(memory_space=pltpu.HBM)
    shape = jax.ShapeDtypeStruct

    def terms_of(b):
        return (2 * b + 3) * tall, 3 * NB

    if last:
        outs, specs = [shape((padded, size), jnp.float32)], [vmem]
    else:
        outs = [
            shape((padded, wide), jnp.float32),
            shape(terms_of(c), jnp.bfloat16),
            shape((tall, wide), jnp.float32),
        ]
        specs = [vmem, hbm, hbm]
        if c == 0:
            outs, specs = [shape((padded + SUB, size), jnp.float32)] + outs, [vmem] + specs
    earlier = [terms for terms, _ in state] + ([w for _, w in state] if last else [])
    return pl.pallas_call(
        functools.partial(panel_kernel, c, size, seqs, padded),
        in_specs=([pl.BlockSpec(memory_space=pltpu.SMEM)] + [vmem] * 6 if c else [vmem]) + [hbm] * len(earlier),
        out_specs=specs,
        out_shape=outs,
        scratch_shapes=[
            pltpu.VMEM((tall + padded, wide), jnp.float32),
            pltpu.VMEM((2, 2 * NB, NB), jnp.float32),
            pltpu.VMEM(terms_of(0 if last else c), jnp.bfloat16),
            pltpu.SemaphoreType.DMA((len(earlier) + 2,)),
        ]
        + [pltpu.VMEM(x.shape, x.dtype) for x in earlier],
        compiler_params=pltpu.CompilerParams(vmem_limit_bytes=40 << 20),
        cost_estimate=pl.CostEstimate(flops=1_200_000_000, bytes_accessed=4_000_000, transcendentals=0),
        name="panel%d" % c,
    )(*inputs, *earlier)


def score_kernel(solved_ref, query_ref, out_ref):
    rows = solved_ref.shape[0]
    terms = by_rows(jnp.concatenate(split(solved_ref[...]), axis=0), query_ref[...])
    out_ref[...] = terms[0:rows] + terms[rows : 2 * rows] + terms[2 * rows :]


def score(solved, queries):
    vmem = pl.BlockSpec(memory_space=pltpu.VMEM)
    return pl.pallas_call(
        score_kernel,
        in_specs=[vmem, vmem],
        out_specs=vmem,
        out_shape=jax.ShapeDtypeStruct((solved.shape[0], queries.shape[0]), jnp.float32),
        name="score",
    )(solved, queries)


def after(x, *others):
    return lax.optimization_barrier((x,) + others)[0]


def inward(n):
    steps = [[(s, s + 1), (n - 1 - s, n - 2 - s)] for s in range(n // 2 - 1)]
    return steps + [[(n // 2 - 1, n // 2), (n // 2, n // 2 - 1)]] if n > 1 else []


def from_middle(x):
    n = lax.axis_size("dp")
    here = lax.axis_index("dp")
    for s in range(n // 2 - 2, -1, -1):
        got = lax.ppermute(x, "dp", [(s + 1, s), (n - 2 - s, n - 1 - s)])
        x = jnp.where((here == s) | (here == n - 1 - s), got, x)
    return x


SWAP = [(0, 1), (1, 0)]


def body(activations, out_grads, proj_in, proj_out, seq_lengths, fisher_prior, query_grads):
    tok_half = activations.shape[2]
    prior = fisher_prior[0, 0]
    size = prior.shape[0]
    seqs = lax.axis_size("dp")
    rep, dp = lax.axis_index("rep"), lax.axis_index("dp")
    count = size // (2 * NB)
    steps = inward(seqs)

    def over_rep(c, gate):
        top, wide = 2 * c * NB, 2 * (c + 1) * NB
        array = prior if gate is None else after(prior, gate)
        other = lax.dynamic_slice(array, (top + (1 - rep) * NB, 0), (NB, wide))
        own = lax.dynamic_slice(array, (top + rep * NB, 0), (NB, wide))
        return own, lax.ppermute(other, "rep", SWAP)

    second = over_rep(1, None)
    place = jnp.stack([rep * tok_half, seq_lengths[0], dp]).astype(jnp.int32)
    first = project(place, seqs, activations, out_grads, proj_in, proj_out, fisher_prior)
    first = first + lax.ppermute(first, "rep", SWAP)
    swapped = came = first
    for i, step in enumerate(steps):
        first = first + lax.ppermute(first, "dp", step)
        if i == 0:
            came = first
    sums = [None, after(second[0] + second[1], came)]
    sums += [after(sum(over_rep(c, swapped)), came) for c in range(2, count)]
    queries = lax.all_gather(after(query_grads[0, 0], first), "dp", axis=0, tiled=True)
    aux, x_rows, *out = panel(0, size, seqs, [after(first, *sums[1:])], [])
    state, gates = [out], [aux]
    place = rep.astype(jnp.int32).reshape(1)
    for c in range(1, count):
        x, got = sums[c], jnp.zeros_like(sums[c])
        for i, step in enumerate(steps):
            if i:
                x = x + got
            got = lax.ppermute(x, "dp", step)
            if i < len(steps) - 1 and c > 1:
                got = after(got, gates[c - 2])
        got = after(got, gates[c - 1])
        others = [lax.ppermute(half, "rep", SWAP) for half in (x, got)]
        out = panel(c, size, seqs, [place, x, got, *others, aux, x_rows], state)
        gates.append(out[0])
        if c < count - 1:
            x_rows, *out = out
            state.append(out)
    scores = from_middle(score(out[0], queries))
    mine = lax.dynamic_slice(scores, (dp, 0), (1, scores.shape[1]))
    if lax.axis_size("mod") == 2:
        return mine + lax.ppermute(mine, "mod", SWAP)
    return lax.psum(mine, "mod")


def solution(mesh):
    placed = (
        P("mod", ("grp", "dp"), "rep", None),
        P("mod", ("grp", "dp"), "rep", None),
        P("mod", None, None),
        P("mod", None, None),
        P(("grp", "dp")),
        P("mod", ("grp", "dp", "rep"), None, None),
        P("mod", "rep", "dp", None),
    )
    return jax.shard_map(
        body, mesh=mesh, in_specs=placed, out_specs=P(("grp", "dp"), "rep"), check_vma=False
    )
```

```python
import functools

import jax
import jax.numpy as jnp
from jax import lax
from jax.experimental import pallas as pl
from jax.experimental.pallas import tpu as pltpu
from jax.sharding import PartitionSpec as P

damping_frac = 0.01
NB = 128
LANES = 128
SUB = 8
HEIGHTS = (1, 2, 2, 2, 1)
STARTS = tuple(sum(HEIGHTS[:c]) for c in range(len(HEIGHTS)))
HIGH = lax.Precision.HIGHEST


def iota(shape, dim):
    return lax.broadcasted_iota(jnp.int32, shape, dim)


def dot(a, b, dims, precision=HIGH):
    return lax.dot_general(
        a, b, (dims, ((), ())), precision=precision, preferred_element_type=jnp.float32
    )


def split(x):
    one = x.astype(jnp.bfloat16)
    x = x - one.astype(jnp.float32)
    two = x.astype(jnp.bfloat16)
    three = (x - two.astype(jnp.float32)).astype(jnp.bfloat16)
    return one, two, three


def left_terms(x):
    one, two, three = split(x)
    return jnp.concatenate([one, one, two, two, one, three], axis=1)


def right_terms(x):
    one, two, three = split(x)
    return jnp.concatenate([one, two, one, two, three, one], axis=1)


def three_terms(x):
    return jnp.concatenate(split(x), axis=1)


def right_six(x):
    one, two, three = x[:, :NB], x[:, NB : 2 * NB], x[:, 2 * NB :]
    return jnp.concatenate([one, two, one, two, three, one], axis=1)


def by_rows(a, b):
    return dot(a, b, ((1,), (1,)), None)


def project_kernel(steps, seqs, place_ref, act_ref, grad_ref, pin_ref, pout_ref, prior_ref, out_ref, ins, outs, tr):
    step = pl.program_id(0)
    in_side = by_rows(act_ref[0, 0], pin_ref[0])
    out_side = by_rows(grad_ref[0, 0], pout_ref[0])
    block = prior_ref[0, 0]
    on_diag = iota(block.shape, 0) == iota(block.shape, 1)
    line = jnp.sum(jnp.where(on_diag, block, 0.0), axis=0, keepdims=True)
    line = sum(line[:, c : c + LANES] for c in range(0, block.shape[1], LANES))

    @pl.when(step == 0)
    def _():
        ins[...] = in_side
        outs[...] = out_side
        tr[...] = jnp.zeros_like(tr)
        tr[0:1, :] = line
        out_ref[out_ref.shape[0] - NB :, :] = block[0:NB, 0:NB]

    @pl.when(step > 0)
    def _():
        ins[...] += in_side
        outs[...] += out_side
        tr[0:1, :] += line

    @pl.when(step == steps - 1)
    def _():
        rank = ins.shape[1]
        fold = LANES // rank
        rows = rank // fold
        token = place_ref[0] + iota(outs.shape, 0)
        kept = jnp.where(token < place_ref[1], outs[...], 0.0)
        matrix = dot(kept, ins[...], ((0,), (0,)))
        matrix = jnp.concatenate([matrix] * fold, axis=1)
        o = iota((rank, LANES), 0)
        lane = iota((rank, LANES), 1)
        matrix = jnp.where(lax.rem(o, fold) == lane // rank, matrix, 0.0)
        pick = (iota((rows, rank), 1) // fold == iota((rows, rank), 0)).astype(jnp.float32)
        vector = dot(pick, matrix, ((1,), (0,)))
        for s in range(seqs):
            out_ref[s * rows : (s + 1) * rows, :] = jnp.where(place_ref[2] == s, vector, 0.0)
        out_ref[seqs * rows : (seqs + 1) * rows, :] = tr[...]


def project(place, seqs, activations, out_grads, proj_in, proj_out, fisher_prior):
    steps = 4
    tok, width = activations.shape[2:]
    rank = proj_in.shape[1]
    size = fisher_prior.shape[2]
    part, blk = width // steps, size // steps
    rows = size // LANES
    height = (seqs + 1) * rows + NB
    return pl.pallas_call(
        functools.partial(project_kernel, steps, seqs),
        grid=(steps,),
        in_specs=[
            pl.BlockSpec(memory_space=pltpu.SMEM),
            pl.BlockSpec((1, 1, tok, part), lambda i: (0, 0, 0, i)),
            pl.BlockSpec((1, 1, tok, part), lambda i: (0, 0, 0, i)),
            pl.BlockSpec((1, rank, part), lambda i: (0, 0, i)),
            pl.BlockSpec((1, rank, part), lambda i: (0, 0, i)),
            pl.BlockSpec((1, 1, blk, blk), lambda i: (0, 0, i, i)),
        ],
        out_specs=pl.BlockSpec((height, LANES), lambda i: (0, 0)),
        out_shape=jax.ShapeDtypeStruct((height, LANES), jnp.float32),
        scratch_shapes=[
            pltpu.VMEM((tok, rank), jnp.float32),
            pltpu.VMEM((tok, rank), jnp.float32),
            pltpu.VMEM((rows, LANES), jnp.float32),
        ],
        compiler_params=pltpu.CompilerParams(vmem_limit_bytes=60 << 20),
        name="project",
    )(place, activations, out_grads, proj_in, proj_out, fisher_prior)


def reciprocal(p):
    return pl.reciprocal(p, approx=True)


def spread(x, k):
    return jnp.broadcast_to(x[k : k + 1, :], x.shape)


def lanes_of(x, k):
    return jnp.broadcast_to(x[:, k : k + 1], x.shape)


def solve_group(s, sets):
    s = [list(row) for row in s]
    sets = [list(x) for x in sets]
    scaled = [[None] * SUB for _ in sets]
    pairs = []
    for k in range(0, SUB, 2):
        a, b, c = s[k][k], s[k + 1][k], s[k + 1][k + 1]
        r = reciprocal(a * c - b * b)
        rest = range(k + 2, SUB)
        m = {i: s[i][k] * c - s[i][k + 1] * b for i in rest}
        n = {i: s[i][k + 1] * a - s[i][k] * b for i in rest}
        for i in rest:
            for j in range(k + 2, i + 1):
                s[i][j] = s[i][j] - (m[i] * s[j][k] + n[i] * s[j][k + 1]) * r
        m = {i: m[i] * r for i in rest}
        n = {i: n[i] * r for i in rest}
        for x, y in zip(sets, scaled):
            y[k], y[k + 1] = (c * x[k] - b * x[k + 1]) * r, (a * x[k + 1] - b * x[k]) * r
            for i in rest:
                x[i] = x[i] - (m[i] * x[k] + n[i] * x[k + 1])
        pairs.append((m, n))
    return sets, scaled, pairs


def back_group(w, pairs):
    w = list(w)
    for k in range(SUB - 4, -1, -2):
        m, n = pairs[k // 2]
        for i in range(SUB - 2, k, -2):
            w[k] = w[k] - (m[i] * w[i] + m[i + 1] * w[i + 1])
            w[k + 1] = w[k + 1] - (n[i] * w[i] + n[i + 1] * w[i + 1])
    return w


def less_products(x, a, b):
    early = (a[0] * b[0] + a[1] * b[1]) + (a[2] * b[2] + a[3] * b[3])
    return (x - early) - (a[4] * b[4] + a[5] * b[5]) - (a[6] * b[6] + a[7] * b[7])


def eliminate(rows):
    groups = len(rows)
    rows = list(rows)
    sub = iota((SUB, LANES), 0)
    lane = iota((SUB, LANES), 1)
    lower, scaled_rows = [], []
    cols = [lanes_of(rows[0], j) for j in range(SUB)]
    for g in range(groups):
        first = g * SUB
        here = (lane >= first) & (lane < first + SUB)
        unit = (lane - first == sub).astype(jnp.float32)
        s = [[spread(cols[j], i) for j in range(i + 1)] for i in range(SUB)]
        work = jnp.where(here, unit, rows[g])
        lower.append(jnp.where(lane < first + SUB, work, 0.0))
        near = list(range(g + 1, min(g + 3, groups)))
        sets = [[lanes_of(rows[h], first + j) for j in range(SUB)] for h in near]
        if near:
            ahead = [lanes_of(rows[g + 1], first + SUB + j) for j in range(SUB)]
        sets, scaled, pairs = solve_group(s, sets + [[spread(work, i) for i in range(SUB)]])
        if near:
            cols = [less_products(ahead[j], sets[0], [spread(d, j) for d in scaled[0]]) for j in range(SUB)]
        for h, x in zip(near, sets):
            rows[h] = less_products(jnp.where(here, 0.0, rows[h]), x, scaled[-1])
        picks = back_group(scaled[-1], pairs)
        work = picks[0]
        for i in range(1, SUB):
            work = jnp.where(sub == i, picks[i], work)
        scaled_rows.append(jnp.where(lane < first + SUB, work, 0.0))
        for h in range(g + 3, groups):
            x = [lanes_of(rows[h], first + j) for j in range(SUB)]
            rows[h] = less_products(jnp.where(here, 0.0, rows[h]), x[::-1], picks[::-1])
    return lower, scaled_rows


def owner(k):
    return max(b for b in range(len(STARTS)) if STARTS[b] <= k)


def y_rows(b, k):
    return HEIGHTS[b] * 2 * NB + k * HEIGHTS[b] * NB


def panel_kernel(c, size, seqs, padded, *refs):
    refs = list(refs)
    tall, done = HEIGHTS[c] * NB, STARTS[c] * NB
    wide = done + tall
    last = wide == size
    waits = {}

    def start(name, source, target, sem):
        waits[name] = pltpu.make_async_copy(source, target, sem)
        waits[name].start()

    def wait(name):
        if name in waits:
            waits.pop(name).wait()

    if c == 0:
        first_ref = refs.pop(0)
        head = first_ref.shape[0] - NB
        rows = size // LANES
    else:
        place_ref, half_ref, got_ref, half_other_ref, got_other_ref, aux_ref, x_ref = refs[:7]
        del refs[:7]
    kept = c + (c if last else 0)
    given = refs[:kept]
    del refs[:kept]
    if last:
        out_ref = refs.pop(0)
    else:
        if c == 0:
            aux_ref = refs.pop(0)
        x_out, terms_out, w_out = refs[:3]
        del refs[:3]
    p, ef, terms, sems = refs[:4]
    held = refs[4:]
    for b in range(kept):
        start(("terms", b) if b < c else ("w", b - c), given[b], held[b], sems.at[b])

    if c == 0:
        if padded > seqs:
            aux_ref[seqs:padded, :] = jnp.zeros((padded - seqs, size), jnp.float32)
        for r in range(seqs * rows):
            at = r % rows * LANES
            aux_ref[r // rows : r // rows + 1, at : at + LANES] = first_ref[r : r + 1, :]
        v = aux_ref[0:padded, :]
        trace = jnp.sum(first_ref[seqs * rows : head, :]) + jnp.sum(v * v)
        aux_ref[padded:, :] = size / jnp.broadcast_to(trace, (SUB, size))
    scale = aux_ref[padded : padded + 1, :]
    one, two, three = split(aux_ref[0:padded, 0:wide])
    outer_left = jnp.concatenate([x[:, done:] for x in (one, one, two, two, one, three)], axis=0)
    outer_right = jnp.concatenate([one, two, one, two, three, one], axis=0)
    if c == 0:
        p[0:NB, :] = first_ref[head:, :]
    else:
        rep, half = place_ref[0], tall // 2
        p[pl.ds(pl.multiple_of(rep * half, half), half), :] = half_ref[...] + got_ref[...]
        p[pl.ds(pl.multiple_of((1 - rep) * half, half), half), :] = half_other_ref[...] + got_other_ref[...]
    outer = dot(outer_left, outer_right, ((0,), (0,)), None)
    eye = iota((tall, wide), 0) + done == iota((tall, wide), 1)
    p[0:tall, :] = (p[0:tall, :] + outer) * scale[:, 0:wide] + jnp.where(eye, damping_frac, 0.0)
    if c:
        p[tall:, 0:done] = x_ref[...]
    p[tall:, done:] = aux_ref[0:padded, done:wide]

    for k in range(STARTS[c]):
        at, end = k * NB, (k + 1) * NB
        b = owner(k)
        wait(("terms", b))
        both = right_six(held[b][(k - STARTS[b]) * 2 * NB : (k - STARTS[b] + 1) * 2 * NB, :])
        y = by_rows(left_terms(p[0:tall, at:end]), both)
        p[0:tall, at:end] = y[:, NB:]
        left = left_terms(p[:, at:end])
        if not last:
            terms[y_rows(c, k) : y_rows(c, k) + tall, :] = three_terms(y[:, :NB])
        for b in range(owner(k), c):
            skip = max(k + 1 - STARTS[b], 0) * NB
            if skip < HEIGHTS[b] * NB:
                wait(("terms", b))
                cols = slice(STARTS[b] * NB + skip, (STARTS[b] + HEIGHTS[b]) * NB)
                right = right_six(held[b][y_rows(b, k) + skip : y_rows(b, k) + HEIGHTS[b] * NB, :])
                p[0:tall, cols] -= by_rows(left[0:tall], right)
        p[:, done:] -= by_rows(left, right_terms(y[:, :NB]))
    for i in range(HEIGHTS[c]):
        at, end = done + i * NB, done + (i + 1) * NB
        low, scl = eliminate([p[i * NB + r : i * NB + r + SUB, at:end] for r in range(0, NB, SUB)])
        for r in range(NB // SUB):
            ef[i, r * SUB : (r + 1) * SUB, :] = low[r]
            ef[i, NB + r * SUB : NB + (r + 1) * SUB, :] = scl[r]
        if not last:
            terms[i * 2 * NB : (i + 1) * 2 * NB, :] = three_terms(ef[i])
        both = right_terms(ef[i])
        rest = (i + 1) * NB
        y = by_rows(left_terms(p[rest:, at:end]), both)
        p[rest:, at:end] = y[:, NB:]
        if rest < tall:
            if not last:
                top = y_rows(c, STARTS[c] + i)
                terms[top : top + rest, :] = jnp.zeros((rest, 3 * NB), jnp.bfloat16)
                terms[top + rest : top + tall, :] = three_terms(y[0 : tall - rest, :NB])
            p[rest:, end:] -= by_rows(left_terms(y[:, NB:]), right_terms(y[0 : tall - rest, :NB]))
    if not last:
        x_out[...] = p[tall:, :]
        start("terms", terms, terms_out, sems.at[kept])
        start("w", p.at[0:tall, :], w_out, sems.at[kept + 1])
        wait("terms")
        wait("w")
        return
    for k in range(size // NB - 1, -1, -1):
        at, end = k * NB, (k + 1) * NB
        b = owner(k)
        i = k - STARTS[b]
        row = i * NB
        if b == c:
            e, w = ef[i, 0:NB, :], p[row : row + NB, 0:at]
        else:
            e = held[b][2 * row : 2 * row + NB, :].astype(jnp.float32)
            e = e[:, :NB] + e[:, NB : 2 * NB] + e[:, 2 * NB :]
            wait(("w", b))
            w = held[c + b][row : row + NB, 0:at]
        z = dot(p[tall:, at:end], e, ((1,), (0,)))
        p[tall:, at:end] = z
        if k:
            p[tall:, 0:at] -= dot(z, w, ((1,), (0,)))
    out_ref[...] = p[tall:, :] * scale


def panel(c, size, seqs, inputs, state):
    padded = -(-seqs // SUB) * SUB
    tall = HEIGHTS[c] * NB
    wide = STARTS[c] * NB + tall
    last = wide == size
    vmem, hbm = pl.BlockSpec(memory_space=pltpu.VMEM), pl.BlockSpec(memory_space=pltpu.HBM)
    shape = jax.ShapeDtypeStruct

    def terms_of(b):
        return y_rows(b, STARTS[b] + HEIGHTS[b] - 1), 3 * NB

    if last:
        outs, specs = [shape((padded, size), jnp.float32)], [vmem]
    else:
        outs = [
            shape((padded, wide), jnp.float32),
            shape(terms_of(c), jnp.bfloat16),
            shape((tall, wide), jnp.float32),
        ]
        specs = [vmem, hbm, hbm]
        if c == 0:
            outs, specs = [shape((padded + SUB, size), jnp.float32)] + outs, [vmem] + specs
    earlier = [terms for terms, _ in state] + ([w for _, w in state] if last else [])
    return pl.pallas_call(
        functools.partial(panel_kernel, c, size, seqs, padded),
        in_specs=([pl.BlockSpec(memory_space=pltpu.SMEM)] + [vmem] * 6 if c else [vmem]) + [hbm] * len(earlier),
        out_specs=specs,
        out_shape=outs,
        scratch_shapes=[
            pltpu.VMEM((tall + padded, wide), jnp.float32),
            pltpu.VMEM((HEIGHTS[c], 2 * NB, NB), jnp.float32),
            pltpu.VMEM(terms_of(0 if last else c), jnp.bfloat16),
            pltpu.SemaphoreType.DMA((len(earlier) + 2,)),
        ]
        + [pltpu.VMEM(x.shape, x.dtype) for x in earlier],
        compiler_params=pltpu.CompilerParams(vmem_limit_bytes=40 << 20),
        cost_estimate=pl.CostEstimate(flops=1_200_000_000, bytes_accessed=4_000_000, transcendentals=0),
        name="panel%d" % c,
    )(*inputs, *earlier)


def score_kernel(solved_ref, query_ref, out_ref):
    rows = solved_ref.shape[0]
    terms = by_rows(jnp.concatenate(split(solved_ref[...]), axis=0), query_ref[...])
    out_ref[...] = terms[0:rows] + terms[rows : 2 * rows] + terms[2 * rows :]


def score(solved, queries):
    vmem = pl.BlockSpec(memory_space=pltpu.VMEM)
    return pl.pallas_call(
        score_kernel,
        in_specs=[vmem, vmem],
        out_specs=vmem,
        out_shape=jax.ShapeDtypeStruct((solved.shape[0], queries.shape[0]), jnp.float32),
        name="score",
    )(solved, queries)


def after(x, *others):
    return lax.optimization_barrier((x,) + others)[0]


def inward(n):
    steps = [[(s, s + 1), (n - 1 - s, n - 2 - s)] for s in range(n // 2 - 1)]
    return steps + [[(n // 2 - 1, n // 2), (n // 2, n // 2 - 1)]] if n > 1 else []


def from_middle(x):
    n = lax.axis_size("dp")
    here = lax.axis_index("dp")
    for s in range(n // 2 - 2, -1, -1):
        got = lax.ppermute(x, "dp", [(s + 1, s), (n - 2 - s, n - 1 - s)])
        x = jnp.where((here == s) | (here == n - 1 - s), got, x)
    return x


SWAP = [(0, 1), (1, 0)]


def body(activations, out_grads, proj_in, proj_out, seq_lengths, fisher_prior, query_grads):
    tok_half = activations.shape[2]
    prior = fisher_prior[0, 0]
    size = prior.shape[0]
    seqs = lax.axis_size("dp")
    rep, dp = lax.axis_index("rep"), lax.axis_index("dp")
    count = len(HEIGHTS)
    steps = inward(seqs)

    def over_rep(c, gate):
        top, half = STARTS[c] * NB, HEIGHTS[c] * NB // 2
        wide = top + 2 * half
        array = prior if gate is None else after(prior, gate)
        other = lax.dynamic_slice(array, (top + (1 - rep) * half, 0), (half, wide))
        own = lax.dynamic_slice(array, (top + rep * half, 0), (half, wide))
        return own, lax.ppermute(other, "rep", SWAP)

    second = over_rep(1, None)
    place = jnp.stack([rep * tok_half, seq_lengths[0], dp]).astype(jnp.int32)
    first = project(place, seqs, activations, out_grads, proj_in, proj_out, fisher_prior)
    first = first + lax.ppermute(first, "rep", SWAP)
    swapped = came = first
    for i, step in enumerate(steps):
        first = first + lax.ppermute(first, "dp", step)
        if i == 0:
            came = first
    sums = [None, after(second[0] + second[1], came)]
    sums += [after(sum(over_rep(c, swapped)), came) for c in range(2, count)]
    aux, x_rows, *out = panel(0, size, seqs, [after(first, *sums[1:])], [])
    state, gates = [out], [aux]
    place = rep.astype(jnp.int32).reshape(1)

    def inwards(x, gate):
        for step in steps[:-1]:
            x = x + after(lax.ppermute(x, "dp", step), gate)
        return x

    inner = [None, inwards(sums[1], came), inwards(sums[2], gates[0])]
    for c in range(1, count):
        if c == 2:
            inner += [inwards(x, gates[1]) for x in sums[3:]]
        x = inner[c]
        got = lax.ppermute(x, "dp", steps[-1]) if steps else jnp.zeros_like(x)
        if c == count - 3:
            x = after(x, inner[-1])
        got = after(got, gates[c - 1])
        others = [lax.ppermute(half, "rep", SWAP) for half in (x, got)]
        out = panel(c, size, seqs, [place, x, got, *others, aux, x_rows], state)
        gates.append(out[0])
        if c == 2:
            queries = lax.all_gather(after(query_grads[0, 0], out[0]), "dp", axis=0, tiled=True)
        if c < count - 1:
            x_rows, *out = out
            state.append(out)
    scores = from_middle(score(out[0], queries))
    mine = lax.dynamic_slice(scores, (dp, 0), (1, scores.shape[1]))
    if lax.axis_size("mod") == 2:
        return mine + lax.ppermute(mine, "mod", SWAP)
    return lax.psum(mine, "mod")


def solution(mesh):
    placed = (
        P("mod", ("grp", "dp"), "rep", None),
        P("mod", ("grp", "dp"), "rep", None),
        P("mod", None, None),
        P("mod", None, None),
        P(("grp", "dp")),
        P("mod", ("grp", "dp", "rep"), None, None),
        P("mod", "rep", "dp", None),
    )
    return jax.shard_map(
        body, mesh=mesh, in_specs=placed, out_specs=P(("grp", "dp"), "rep"), check_vma=False
    )
```

```python
import functools

import jax
import jax.numpy as jnp
from jax import lax
from jax.experimental import pallas as pl
from jax.experimental.pallas import tpu as pltpu
from jax.sharding import PartitionSpec as P

damping_frac = 0.01
NB = 128
LANES = 128
SUB = 8
HEIGHTS = (1, 2, 2, 2, 1)
STARTS = tuple(sum(HEIGHTS[:c]) for c in range(len(HEIGHTS)))
HIGH = lax.Precision.HIGHEST


def iota(shape, dim):
    return lax.broadcasted_iota(jnp.int32, shape, dim)


def dot(a, b, dims, precision=HIGH):
    return lax.dot_general(
        a, b, (dims, ((), ())), precision=precision, preferred_element_type=jnp.float32
    )


def split(x):
    one = x.astype(jnp.bfloat16)
    x = x - one.astype(jnp.float32)
    two = x.astype(jnp.bfloat16)
    three = (x - two.astype(jnp.float32)).astype(jnp.bfloat16)
    return one, two, three


def left_terms(x):
    one, two, three = split(x)
    return jnp.concatenate([one, one, two, two, one, three], axis=1)


def right_terms(x):
    one, two, three = split(x)
    return jnp.concatenate([one, two, one, two, three, one], axis=1)


def three_terms(x):
    return jnp.concatenate(split(x), axis=1)


def right_six(x):
    one, two, three = x[:, :NB], x[:, NB : 2 * NB], x[:, 2 * NB :]
    return jnp.concatenate([one, two, one, two, three, one], axis=1)


def by_rows(a, b):
    return dot(a, b, ((1,), (1,)), None)


def project_kernel(steps, seqs, place_ref, act_ref, grad_ref, pin_ref, pout_ref, prior_ref, out_ref, ins, outs, tr):
    step = pl.program_id(0)
    in_side = by_rows(act_ref[0, 0], pin_ref[0])
    out_side = by_rows(grad_ref[0, 0], pout_ref[0])
    block = prior_ref[0, 0]
    on_diag = iota(block.shape, 0) == iota(block.shape, 1)
    line = jnp.sum(jnp.where(on_diag, block, 0.0), axis=0, keepdims=True)
    line = sum(line[:, c : c + LANES] for c in range(0, block.shape[1], LANES))

    @pl.when(step == 0)
    def _():
        ins[...] = in_side
        outs[...] = out_side
        tr[...] = jnp.zeros_like(tr)
        tr[0:1, :] = line
        out_ref[out_ref.shape[0] - NB :, :] = block[0:NB, 0:NB]

    @pl.when(step > 0)
    def _():
        ins[...] += in_side
        outs[...] += out_side
        tr[0:1, :] += line

    @pl.when(step == steps - 1)
    def _():
        rank = ins.shape[1]
        fold = LANES // rank
        rows = rank // fold
        token = place_ref[0] + iota(outs.shape, 0)
        kept = jnp.where(token < place_ref[1], outs[...], 0.0)
        matrix = dot(kept, ins[...], ((0,), (0,)))
        matrix = jnp.concatenate([matrix] * fold, axis=1)
        o = iota((rank, LANES), 0)
        lane = iota((rank, LANES), 1)
        matrix = jnp.where(lax.rem(o, fold) == lane // rank, matrix, 0.0)
        pick = (iota((rows, rank), 1) // fold == iota((rows, rank), 0)).astype(jnp.float32)
        vector = dot(pick, matrix, ((1,), (0,)))
        for s in range(seqs):
            out_ref[s * rows : (s + 1) * rows, :] = jnp.where(place_ref[2] == s, vector, 0.0)
        out_ref[seqs * rows : (seqs + 1) * rows, :] = tr[...]


def project(place, seqs, activations, out_grads, proj_in, proj_out, fisher_prior):
    steps = 4
    tok, width = activations.shape[2:]
    rank = proj_in.shape[1]
    size = fisher_prior.shape[2]
    part, blk = width // steps, size // steps
    rows = size // LANES
    height = (seqs + 1) * rows + NB
    return pl.pallas_call(
        functools.partial(project_kernel, steps, seqs),
        grid=(steps,),
        in_specs=[
            pl.BlockSpec(memory_space=pltpu.SMEM),
            pl.BlockSpec((1, 1, tok, part), lambda i: (0, 0, 0, i)),
            pl.BlockSpec((1, 1, tok, part), lambda i: (0, 0, 0, i)),
            pl.BlockSpec((1, rank, part), lambda i: (0, 0, i)),
            pl.BlockSpec((1, rank, part), lambda i: (0, 0, i)),
            pl.BlockSpec((1, 1, blk, blk), lambda i: (0, 0, i, i)),
        ],
        out_specs=pl.BlockSpec((height, LANES), lambda i: (0, 0)),
        out_shape=jax.ShapeDtypeStruct((height, LANES), jnp.float32),
        scratch_shapes=[
            pltpu.VMEM((tok, rank), jnp.float32),
            pltpu.VMEM((tok, rank), jnp.float32),
            pltpu.VMEM((rows, LANES), jnp.float32),
        ],
        compiler_params=pltpu.CompilerParams(vmem_limit_bytes=60 << 20),
        name="project",
    )(place, activations, out_grads, proj_in, proj_out, fisher_prior)


def reciprocal(p):
    return pl.reciprocal(p, approx=True)


def spread(x, k):
    return jnp.broadcast_to(x[k : k + 1, :], x.shape)


def lanes_of(x, k):
    return jnp.broadcast_to(x[:, k : k + 1], x.shape)


def solve_group(s, sets):
    s = [list(row) for row in s]
    sets = [list(x) for x in sets]
    scaled = [[None] * SUB for _ in sets]
    pairs = []
    for k in range(0, SUB, 2):
        a, b, c = s[k][k], s[k + 1][k], s[k + 1][k + 1]
        r = reciprocal(a * c - b * b)
        rest = range(k + 2, SUB)
        m = {i: s[i][k] * c - s[i][k + 1] * b for i in rest}
        n = {i: s[i][k + 1] * a - s[i][k] * b for i in rest}
        for i in rest:
            for j in range(k + 2, i + 1):
                s[i][j] = s[i][j] - (m[i] * s[j][k] + n[i] * s[j][k + 1]) * r
        m = {i: m[i] * r for i in rest}
        n = {i: n[i] * r for i in rest}
        for x, y in zip(sets, scaled):
            y[k], y[k + 1] = (c * x[k] - b * x[k + 1]) * r, (a * x[k + 1] - b * x[k]) * r
            for i in rest:
                x[i] = x[i] - (m[i] * x[k] + n[i] * x[k + 1])
        pairs.append((m, n))
    return sets, scaled, pairs


def back_group(w, pairs):
    w = list(w)
    for k in range(SUB - 4, -1, -2):
        m, n = pairs[k // 2]
        for i in range(SUB - 2, k, -2):
            w[k] = w[k] - (m[i] * w[i] + m[i + 1] * w[i + 1])
            w[k + 1] = w[k + 1] - (n[i] * w[i] + n[i + 1] * w[i + 1])
    return w


def less_products(x, a, b):
    early = (a[0] * b[0] + a[1] * b[1]) + (a[2] * b[2] + a[3] * b[3])
    return (x - early) - (a[4] * b[4] + a[5] * b[5]) - (a[6] * b[6] + a[7] * b[7])


def eliminate(rows):
    groups = len(rows)
    rows = list(rows)
    sub = iota((SUB, LANES), 0)
    lane = iota((SUB, LANES), 1)
    lower, scaled_rows = [], []
    cols = [lanes_of(rows[0], j) for j in range(SUB)]
    for g in range(groups):
        first = g * SUB
        here = (lane >= first) & (lane < first + SUB)
        unit = (lane - first == sub).astype(jnp.float32)
        s = [[spread(cols[j], i) for j in range(i + 1)] for i in range(SUB)]
        work = jnp.where(here, unit, rows[g])
        lower.append(jnp.where(lane < first + SUB, work, 0.0))
        near = list(range(g + 1, min(g + 3, groups)))
        sets = [[lanes_of(rows[h], first + j) for j in range(SUB)] for h in near]
        if near:
            ahead = [lanes_of(rows[g + 1], first + SUB + j) for j in range(SUB)]
        sets, scaled, pairs = solve_group(s, sets + [[spread(work, i) for i in range(SUB)]])
        if near:
            cols = [less_products(ahead[j], sets[0], [spread(d, j) for d in scaled[0]]) for j in range(SUB)]
        for h, x in zip(near, sets):
            rows[h] = less_products(jnp.where(here, 0.0, rows[h]), x, scaled[-1])
        picks = back_group(scaled[-1], pairs)
        work = picks[0]
        for i in range(1, SUB):
            work = jnp.where(sub == i, picks[i], work)
        scaled_rows.append(jnp.where(lane < first + SUB, work, 0.0))
        for h in range(g + 3, groups):
            x = [lanes_of(rows[h], first + j) for j in range(SUB)]
            rows[h] = less_products(jnp.where(here, 0.0, rows[h]), x[::-1], picks[::-1])
    return lower, scaled_rows


def owner(k):
    return max(b for b in range(len(STARTS)) if STARTS[b] <= k)


def y_rows(b, k):
    return HEIGHTS[b] * 2 * NB + k * HEIGHTS[b] * NB


def panel_kernel(c, size, seqs, padded, *refs):
    refs = list(refs)
    tall, done = HEIGHTS[c] * NB, STARTS[c] * NB
    wide = done + tall
    last = wide == size
    waits = {}

    def start(name, source, target, sem):
        waits[name] = pltpu.make_async_copy(source, target, sem)
        waits[name].start()

    def wait(name):
        if name in waits:
            waits.pop(name).wait()

    if c == 0:
        first_ref = refs.pop(0)
        head = first_ref.shape[0] - NB
        rows = size // LANES
    else:
        place_ref, half_ref, got_ref, half_other_ref, got_other_ref, aux_ref, x_ref = refs[:7]
        del refs[:7]
    kept = c + (c if last else 0)
    given = refs[:kept]
    del refs[:kept]
    if last:
        out_ref = refs.pop(0)
    else:
        if c == 0:
            aux_ref = refs.pop(0)
        x_out, terms_out, w_out = refs[:3]
        del refs[:3]
    p, ef, terms, sems = refs[:4]
    held = refs[4:]
    for b in range(kept):
        start(("terms", b) if b < c else ("w", b - c), given[b], held[b], sems.at[b])

    if c == 0:
        if padded > seqs:
            aux_ref[seqs:padded, :] = jnp.zeros((padded - seqs, size), jnp.float32)
        for r in range(seqs * rows):
            at = r % rows * LANES
            aux_ref[r // rows : r // rows + 1, at : at + LANES] = first_ref[r : r + 1, :]
        v = aux_ref[0:padded, :]
        trace = jnp.sum(first_ref[seqs * rows : head, :]) + jnp.sum(v * v)
        aux_ref[padded:, :] = size / jnp.broadcast_to(trace, (SUB, size))
    scale = aux_ref[padded : padded + 1, :]
    one, two, three = split(aux_ref[0:padded, 0:wide])
    outer_left = jnp.concatenate([x[:, done:] for x in (one, one, two, two, one, three)], axis=0)
    outer_right = jnp.concatenate([one, two, one, two, three, one], axis=0)
    if c == 0:
        p[0:NB, :] = first_ref[head:, :]
    else:
        rep, half = place_ref[0], tall // 2
        p[pl.ds(pl.multiple_of(rep * half, half), half), :] = half_ref[...] + got_ref[...]
        p[pl.ds(pl.multiple_of((1 - rep) * half, half), half), :] = half_other_ref[...] + got_other_ref[...]
    outer = dot(outer_left, outer_right, ((0,), (0,)), None)
    eye = iota((tall, wide), 0) + done == iota((tall, wide), 1)
    p[0:tall, :] = (p[0:tall, :] + outer) * scale[:, 0:wide] + jnp.where(eye, damping_frac, 0.0)
    if c:
        p[tall:, 0:done] = x_ref[...]
    p[tall:, done:] = aux_ref[0:padded, done:wide]

    for k in range(STARTS[c]):
        at, end = k * NB, (k + 1) * NB
        b = owner(k)
        wait(("terms", b))
        both = right_six(held[b][(k - STARTS[b]) * 2 * NB : (k - STARTS[b] + 1) * 2 * NB, :])
        y = by_rows(left_terms(p[0:tall, at:end]), both)
        p[0:tall, at:end] = y[:, NB:]
        left = left_terms(p[:, at:end])
        if not last:
            terms[y_rows(c, k) : y_rows(c, k) + tall, :] = three_terms(y[:, :NB])
        for b in range(owner(k), c):
            skip = max(k + 1 - STARTS[b], 0) * NB
            if skip < HEIGHTS[b] * NB:
                wait(("terms", b))
                cols = slice(STARTS[b] * NB + skip, (STARTS[b] + HEIGHTS[b]) * NB)
                right = right_six(held[b][y_rows(b, k) + skip : y_rows(b, k) + HEIGHTS[b] * NB, :])
                p[0:tall, cols] -= by_rows(left[0:tall], right)
        p[:, done:] -= by_rows(left, right_terms(y[:, :NB]))
    for i in range(HEIGHTS[c]):
        at, end = done + i * NB, done + (i + 1) * NB
        low, scl = eliminate([p[i * NB + r : i * NB + r + SUB, at:end] for r in range(0, NB, SUB)])
        for r in range(NB // SUB):
            ef[i, r * SUB : (r + 1) * SUB, :] = low[r]
            ef[i, NB + r * SUB : NB + (r + 1) * SUB, :] = scl[r]
        if not last:
            terms[i * 2 * NB : (i + 1) * 2 * NB, :] = three_terms(ef[i])
        both = right_terms(ef[i])
        rest = (i + 1) * NB
        y = by_rows(left_terms(p[rest:, at:end]), both)
        p[rest:, at:end] = y[:, NB:]
        if rest < tall:
            if not last:
                top = y_rows(c, STARTS[c] + i)
                terms[top : top + rest, :] = jnp.zeros((rest, 3 * NB), jnp.bfloat16)
                terms[top + rest : top + tall, :] = three_terms(y[0 : tall - rest, :NB])
            p[rest:, end:] -= by_rows(left_terms(y[:, NB:]), right_terms(y[0 : tall - rest, :NB]))
    if not last:
        x_out[...] = p[tall:, :]
        start("terms", terms, terms_out, sems.at[kept])
        start("w", p.at[0:tall, :], w_out, sems.at[kept + 1])
        wait("terms")
        wait("w")
        return
    for k in range(size // NB - 1, -1, -1):
        at, end = k * NB, (k + 1) * NB
        b = owner(k)
        i = k - STARTS[b]
        row = i * NB
        if b == c:
            e, w = ef[i, 0:NB, :], p[row : row + NB, 0:at]
        else:
            e = held[b][2 * row : 2 * row + NB, :].astype(jnp.float32)
            e = e[:, :NB] + e[:, NB : 2 * NB] + e[:, 2 * NB :]
            wait(("w", b))
            w = held[c + b][row : row + NB, 0:at]
        z = dot(p[tall:, at:end], e, ((1,), (0,)))
        p[tall:, at:end] = z
        if k:
            p[tall:, 0:at] -= dot(z, w, ((1,), (0,)))
    out_ref[...] = p[tall:, :] * scale


def panel(c, size, seqs, inputs, state):
    padded = -(-seqs // SUB) * SUB
    tall = HEIGHTS[c] * NB
    wide = STARTS[c] * NB + tall
    last = wide == size
    vmem, hbm = pl.BlockSpec(memory_space=pltpu.VMEM), pl.BlockSpec(memory_space=pltpu.HBM)
    shape = jax.ShapeDtypeStruct

    def terms_of(b):
        return y_rows(b, STARTS[b] + HEIGHTS[b] - 1), 3 * NB

    if last:
        outs, specs = [shape((padded, size), jnp.float32)], [vmem]
    else:
        outs = [
            shape((padded, wide), jnp.float32),
            shape(terms_of(c), jnp.bfloat16),
            shape((tall, wide), jnp.float32),
        ]
        specs = [vmem, hbm, hbm]
        if c == 0:
            outs, specs = [shape((padded + SUB, size), jnp.float32)] + outs, [vmem] + specs
    earlier = [terms for terms, _ in state] + ([w for _, w in state] if last else [])
    return pl.pallas_call(
        functools.partial(panel_kernel, c, size, seqs, padded),
        in_specs=([pl.BlockSpec(memory_space=pltpu.SMEM)] + [vmem] * 6 if c else [vmem]) + [hbm] * len(earlier),
        out_specs=specs,
        out_shape=outs,
        scratch_shapes=[
            pltpu.VMEM((tall + padded, wide), jnp.float32),
            pltpu.VMEM((HEIGHTS[c], 2 * NB, NB), jnp.float32),
            pltpu.VMEM(terms_of(0 if last else c), jnp.bfloat16),
            pltpu.SemaphoreType.DMA((len(earlier) + 2,)),
        ]
        + [pltpu.VMEM(x.shape, x.dtype) for x in earlier],
        compiler_params=pltpu.CompilerParams(vmem_limit_bytes=40 << 20),
        cost_estimate=pl.CostEstimate(flops=1_200_000_000, bytes_accessed=4_000_000, transcendentals=0),
        name="panel%d" % c,
    )(*inputs, *earlier)


def score_kernel(side_ref, solved_ref, *refs):
    blocks, out_ref = refs[:-1], refs[-1]
    rows = solved_ref.shape[0]
    half = max(len(blocks) // 2, 1)
    count = blocks[0].shape[0]
    solved = jnp.concatenate(split(solved_ref[...]), axis=0)
    for i, block in enumerate(blocks):
        terms = by_rows(solved, block[...])
        low, high = half - 1 - i % half, (half + i % half) if len(blocks) > 1 else 0
        right_side = side_ref[0] if i < half else 1 - side_ref[0]
        at = pl.multiple_of((low + right_side * (high - low)) * count, LANES)
        out_ref[:, pl.ds(at, count)] = terms[0:rows] + terms[rows : 2 * rows] + terms[2 * rows :]


def score(side, solved, blocks):
    vmem = pl.BlockSpec(memory_space=pltpu.VMEM)
    count = len(blocks) * blocks[0].shape[0]
    return pl.pallas_call(
        score_kernel,
        in_specs=[pl.BlockSpec(memory_space=pltpu.SMEM)] + [vmem] * (1 + len(blocks)),
        out_specs=vmem,
        out_shape=jax.ShapeDtypeStruct((solved.shape[0], count), jnp.float32),
        name="score",
    )(side, solved, *blocks)


def after(x, *others):
    return lax.optimization_barrier((x,) + others)[0]


def inward(n):
    steps = [[(s, s + 1), (n - 1 - s, n - 2 - s)] for s in range(n // 2 - 1)]
    return steps + [[(n // 2 - 1, n // 2), (n // 2, n // 2 - 1)]] if n > 1 else []


def from_middle(x):
    n = lax.axis_size("dp")
    here = lax.axis_index("dp")
    for s in range(n // 2 - 2, -1, -1):
        got = lax.ppermute(x, "dp", [(s + 1, s), (n - 2 - s, n - 1 - s)])
        x = jnp.where((here == s) | (here == n - 1 - s), got, x)
    return x


SWAP = [(0, 1), (1, 0)]


def body(activations, out_grads, proj_in, proj_out, seq_lengths, fisher_prior, query_grads):
    tok_half = activations.shape[2]
    prior = fisher_prior[0, 0]
    size = prior.shape[0]
    seqs = lax.axis_size("dp")
    rep, dp = lax.axis_index("rep"), lax.axis_index("dp")
    count = len(HEIGHTS)
    steps = inward(seqs)

    def over_rep(c, gate):
        top, half = STARTS[c] * NB, HEIGHTS[c] * NB // 2
        wide = top + 2 * half
        array = prior if gate is None else after(prior, gate)
        other = lax.dynamic_slice(array, (top + (1 - rep) * half, 0), (half, wide))
        own = lax.dynamic_slice(array, (top + rep * half, 0), (half, wide))
        return own, lax.ppermute(other, "rep", SWAP)

    second = over_rep(1, None)
    place = jnp.stack([rep * tok_half, seq_lengths[0], dp]).astype(jnp.int32)
    first = project(place, seqs, activations, out_grads, proj_in, proj_out, fisher_prior)
    first = first + lax.ppermute(first, "rep", SWAP)
    swapped = came = first
    for i, step in enumerate(steps):
        first = first + lax.ppermute(first, "dp", step)
        if i == 0:
            came = first
    sums = [None, after(second[0] + second[1], came)]
    sums += [after(sum(over_rep(c, swapped)), came) for c in range(2, count)]

    def inwards(x, *gate):
        for step in steps[:-1]:
            x = x + after(lax.ppermute(x, "dp", step), *gate)
        return x

    inner = [None, inwards(sums[1], *sums[2:4])]
    aux, x_rows, *out = panel(0, size, seqs, [after(first, inner[1])], [])
    state, gates = [out], [aux]
    place = rep.astype(jnp.int32).reshape(1)

    inner.append(inwards(sums[2], gates[0]))
    for c in range(1, count):
        if c == 2:
            inner += [inwards(x, gates[1]) for x in sums[3:]]
        x = inner[c]
        got = lax.ppermute(x, "dp", steps[-1]) if steps else jnp.zeros_like(x)
        if c == 2:
            x = after(x, *inner[3:])
        got = after(got, gates[c - 1])
        others = [lax.ppermute(half, "rep", SWAP) for half in (x, got)]
        out = panel(c, size, seqs, [place, x, got, *others, aux, x_rows], state)
        gates.append(out[0])
        if c == 2:
            near = [after(query_grads[0, 0], out[0])]
            for step in steps[:-1]:
                near = near[:1] + [lax.ppermute(x, "dp", step) for x in near]
        if c == 3 and steps:
            near = list(lax.optimization_barrier((*near, out[0])))[:-1]
            near += [lax.ppermute(x, "dp", steps[-1]) for x in near]
        if c < count - 1:
            x_rows, *out = out
            state.append(out)
    side = (dp >= seqs // 2).astype(jnp.int32).reshape(1)
    scores = from_middle(score(side, out[0], near))
    mine = lax.dynamic_slice(scores, (dp, 0), (1, scores.shape[1]))
    if lax.axis_size("mod") == 2:
        return mine + lax.ppermute(mine, "mod", SWAP)
    return lax.psum(mine, "mod")


def solution(mesh):
    placed = (
        P("mod", ("grp", "dp"), "rep", None),
        P("mod", ("grp", "dp"), "rep", None),
        P("mod", None, None),
        P("mod", None, None),
        P(("grp", "dp")),
        P("mod", ("grp", "dp", "rep"), None, None),
        P("mod", "rep", "dp", None),
    )
    return jax.shard_map(
        body, mesh=mesh, in_specs=placed, out_specs=P(("grp", "dp"), "rep"), check_vma=False
    )
```

```python
import functools

import jax
import jax.numpy as jnp
from jax import lax
from jax.experimental import pallas as pl
from jax.experimental.pallas import tpu as pltpu
from jax.sharding import PartitionSpec as P

damping_frac = 0.01
NB = 128
LANES = 128
SUB = 8
HEIGHTS = (1, 2, 2, 2, 1)
STARTS = tuple(sum(HEIGHTS[:c]) for c in range(len(HEIGHTS)))
HIGH = lax.Precision.HIGHEST


def iota(shape, dim):
    return lax.broadcasted_iota(jnp.int32, shape, dim)


def dot(a, b, dims, precision=HIGH):
    return lax.dot_general(
        a, b, (dims, ((), ())), precision=precision, preferred_element_type=jnp.float32
    )


def split(x):
    one = x.astype(jnp.bfloat16)
    x = x - one.astype(jnp.float32)
    two = x.astype(jnp.bfloat16)
    three = (x - two.astype(jnp.float32)).astype(jnp.bfloat16)
    return one, two, three


def left_terms(x):
    one, two, three = split(x)
    return jnp.concatenate([one, one, two, two, one, three], axis=1)


def right_terms(x):
    one, two, three = split(x)
    return jnp.concatenate([one, two, one, two, three, one], axis=1)


def three_terms(x):
    return jnp.concatenate(split(x), axis=1)


def right_six(x):
    one, two, three = x[:, :NB], x[:, NB : 2 * NB], x[:, 2 * NB :]
    return jnp.concatenate([one, two, one, two, three, one], axis=1)


def by_rows(a, b):
    return dot(a, b, ((1,), (1,)), None)


def project_kernel(steps, seqs, place_ref, act_ref, grad_ref, pin_ref, pout_ref, prior_ref, out_ref, ins, outs, tr):
    step = pl.program_id(0)
    in_side = by_rows(act_ref[0, 0], pin_ref[0])
    out_side = by_rows(grad_ref[0, 0], pout_ref[0])
    block = prior_ref[0, 0]
    on_diag = iota(block.shape, 0) == iota(block.shape, 1)
    line = jnp.sum(jnp.where(on_diag, block, 0.0), axis=0, keepdims=True)
    line = sum(line[:, c : c + LANES] for c in range(0, block.shape[1], LANES))

    @pl.when(step == 0)
    def _():
        ins[...] = in_side
        outs[...] = out_side
        tr[...] = jnp.zeros_like(tr)
        tr[0:1, :] = line
        out_ref[out_ref.shape[0] - NB :, :] = block[0:NB, 0:NB]

    @pl.when(step > 0)
    def _():
        ins[...] += in_side
        outs[...] += out_side
        tr[0:1, :] += line

    @pl.when(step == steps - 1)
    def _():
        rank = ins.shape[1]
        fold = LANES // rank
        rows = rank // fold
        token = place_ref[0] + iota(outs.shape, 0)
        kept = jnp.where(token < place_ref[1], outs[...], 0.0)
        matrix = dot(kept, ins[...], ((0,), (0,)))
        matrix = jnp.concatenate([matrix] * fold, axis=1)
        o = iota((rank, LANES), 0)
        lane = iota((rank, LANES), 1)
        matrix = jnp.where(lax.rem(o, fold) == lane // rank, matrix, 0.0)
        pick = (iota((rows, rank), 1) // fold == iota((rows, rank), 0)).astype(jnp.float32)
        vector = dot(pick, matrix, ((1,), (0,)))
        for s in range(seqs):
            out_ref[s * rows : (s + 1) * rows, :] = jnp.where(place_ref[2] == s, vector, 0.0)
        out_ref[seqs * rows : (seqs + 1) * rows, :] = tr[...]


def project(place, seqs, activations, out_grads, proj_in, proj_out, fisher_prior):
    steps = 4
    tok, width = activations.shape[2:]
    rank = proj_in.shape[1]
    size = fisher_prior.shape[2]
    part, blk = width // steps, size // steps
    rows = size // LANES
    height = (seqs + 1) * rows + NB
    return pl.pallas_call(
        functools.partial(project_kernel, steps, seqs),
        grid=(steps,),
        in_specs=[
            pl.BlockSpec(memory_space=pltpu.SMEM),
            pl.BlockSpec((1, 1, tok, part), lambda i: (0, 0, 0, i)),
            pl.BlockSpec((1, 1, tok, part), lambda i: (0, 0, 0, i)),
            pl.BlockSpec((1, rank, part), lambda i: (0, 0, i)),
            pl.BlockSpec((1, rank, part), lambda i: (0, 0, i)),
            pl.BlockSpec((1, 1, blk, blk), lambda i: (0, 0, i, i)),
        ],
        out_specs=pl.BlockSpec((height, LANES), lambda i: (0, 0)),
        out_shape=jax.ShapeDtypeStruct((height, LANES), jnp.float32),
        scratch_shapes=[
            pltpu.VMEM((tok, rank), jnp.float32),
            pltpu.VMEM((tok, rank), jnp.float32),
            pltpu.VMEM((rows, LANES), jnp.float32),
        ],
        compiler_params=pltpu.CompilerParams(vmem_limit_bytes=60 << 20),
        name="project",
    )(place, activations, out_grads, proj_in, proj_out, fisher_prior)


def reciprocal(p):
    return pl.reciprocal(p, approx=True)


def spread(x, k):
    return jnp.broadcast_to(x[k : k + 1, :], x.shape)


def lanes_of(x, k):
    return jnp.broadcast_to(x[:, k : k + 1], x.shape)


def solve_group(s, sets):
    s = [list(row) for row in s]
    sets = [list(x) for x in sets]
    scaled = [[None] * SUB for _ in sets]
    pairs = []
    for k in range(0, SUB, 2):
        a, b, c = s[k][k], s[k + 1][k], s[k + 1][k + 1]
        r = reciprocal(a * c - b * b)
        rest = range(k + 2, SUB)
        m = {i: s[i][k] * c - s[i][k + 1] * b for i in rest}
        n = {i: s[i][k + 1] * a - s[i][k] * b for i in rest}
        for i in rest:
            for j in range(k + 2, i + 1):
                s[i][j] = s[i][j] - (m[i] * s[j][k] + n[i] * s[j][k + 1]) * r
        m = {i: m[i] * r for i in rest}
        n = {i: n[i] * r for i in rest}
        for x, y in zip(sets, scaled):
            y[k], y[k + 1] = (c * x[k] - b * x[k + 1]) * r, (a * x[k + 1] - b * x[k]) * r
            for i in rest:
                x[i] = x[i] - (m[i] * x[k] + n[i] * x[k + 1])
        pairs.append((m, n))
    return sets, scaled, pairs


def back_group(w, pairs):
    w = list(w)
    for k in range(SUB - 4, -1, -2):
        m, n = pairs[k // 2]
        for i in range(SUB - 2, k, -2):
            w[k] = w[k] - (m[i] * w[i] + m[i + 1] * w[i + 1])
            w[k + 1] = w[k + 1] - (n[i] * w[i] + n[i + 1] * w[i + 1])
    return w


def less_products(x, a, b):
    early = (a[0] * b[0] + a[1] * b[1]) + (a[2] * b[2] + a[3] * b[3])
    return (x - early) - (a[4] * b[4] + a[5] * b[5]) - (a[6] * b[6] + a[7] * b[7])


def eliminate(rows):
    groups = len(rows)
    rows = list(rows)
    sub = iota((SUB, LANES), 0)
    lane = iota((SUB, LANES), 1)
    lower, scaled_rows = [], []
    cols = [lanes_of(rows[0], j) for j in range(SUB)]
    for g in range(groups):
        first = g * SUB
        here = (lane >= first) & (lane < first + SUB)
        unit = (lane - first == sub).astype(jnp.float32)
        s = [[spread(cols[j], i) for j in range(i + 1)] for i in range(SUB)]
        work = jnp.where(here, unit, rows[g])
        lower.append(jnp.where(lane < first + SUB, work, 0.0))
        near = list(range(g + 1, min(g + 3, groups)))
        sets = [[lanes_of(rows[h], first + j) for j in range(SUB)] for h in near]
        if near:
            ahead = [lanes_of(rows[g + 1], first + SUB + j) for j in range(SUB)]
        sets, scaled, pairs = solve_group(s, sets + [[spread(work, i) for i in range(SUB)]])
        if near:
            cols = [less_products(ahead[j], sets[0], [spread(d, j) for d in scaled[0]]) for j in range(SUB)]
        for h, x in zip(near, sets):
            rows[h] = less_products(jnp.where(here, 0.0, rows[h]), x, scaled[-1])
        picks = back_group(scaled[-1], pairs)
        work = picks[0]
        for i in range(1, SUB):
            work = jnp.where(sub == i, picks[i], work)
        scaled_rows.append(jnp.where(lane < first + SUB, work, 0.0))
        for h in range(g + 3, groups):
            x = [lanes_of(rows[h], first + j) for j in range(SUB)]
            rows[h] = less_products(jnp.where(here, 0.0, rows[h]), x[::-1], picks[::-1])
    return lower, scaled_rows


def owner(k):
    return max(b for b in range(len(STARTS)) if STARTS[b] <= k)


def y_rows(b, k):
    return HEIGHTS[b] * 2 * NB + k * HEIGHTS[b] * NB


def panel_kernel(c, size, seqs, padded, *refs):
    refs = list(refs)
    tall, done = HEIGHTS[c] * NB, STARTS[c] * NB
    wide = done + tall
    last = wide == size
    waits = {}

    def start(name, source, target, sem):
        waits[name] = pltpu.make_async_copy(source, target, sem)
        waits[name].start()

    def wait(name):
        if name in waits:
            waits.pop(name).wait()

    if c == 0:
        first_ref = refs.pop(0)
        head = first_ref.shape[0] - NB
        rows = size // LANES
    else:
        place_ref, half_ref, got_ref, half_other_ref, got_other_ref, aux_ref, x_ref = refs[:7]
        del refs[:7]
    kept = c + (c if last else 0)
    given = refs[:kept]
    del refs[:kept]
    if last:
        out_ref = refs.pop(0)
    else:
        if c == 0:
            aux_ref = refs.pop(0)
        x_out, terms_out, w_out = refs[:3]
        del refs[:3]
    p, ef, terms, sems = refs[:4]
    held = refs[4:]
    for b in range(kept):
        start(("terms", b) if b < c else ("w", b - c), given[b], held[b], sems.at[b])

    if c == 0:
        if padded > seqs:
            aux_ref[seqs:padded, :] = jnp.zeros((padded - seqs, size), jnp.float32)
        for r in range(seqs * rows):
            at = r % rows * LANES
            aux_ref[r // rows : r // rows + 1, at : at + LANES] = first_ref[r : r + 1, :]
        v = aux_ref[0:padded, :]
        trace = jnp.sum(first_ref[seqs * rows : head, :]) + jnp.sum(v * v)
        aux_ref[padded:, :] = size / jnp.broadcast_to(trace, (SUB, size))
    scale = aux_ref[padded : padded + 1, :]
    one, two, three = split(aux_ref[0:padded, 0:wide])
    outer_left = jnp.concatenate([x[:, done:] for x in (one, one, two, two, one, three)], axis=0)
    outer_right = jnp.concatenate([one, two, one, two, three, one], axis=0)
    if c == 0:
        p[0:NB, :] = first_ref[head:, :]
    else:
        rep, half = place_ref[0], tall // 2
        p[pl.ds(pl.multiple_of(rep * half, half), half), :] = half_ref[...] + got_ref[...]
        p[pl.ds(pl.multiple_of((1 - rep) * half, half), half), :] = half_other_ref[...] + got_other_ref[...]
    outer = dot(outer_left, outer_right, ((0,), (0,)), None)
    eye = iota((tall, wide), 0) + done == iota((tall, wide), 1)
    p[0:tall, :] = (p[0:tall, :] + outer) * scale[:, 0:wide] + jnp.where(eye, damping_frac, 0.0)
    if c:
        p[tall:, 0:done] = x_ref[...]
    p[tall:, done:] = aux_ref[0:padded, done:wide]

    for k in range(STARTS[c]):
        at, end = k * NB, (k + 1) * NB
        b = owner(k)
        wait(("terms", b))
        both = right_six(held[b][(k - STARTS[b]) * 2 * NB : (k - STARTS[b] + 1) * 2 * NB, :])
        y = by_rows(left_terms(p[0:tall, at:end]), both)
        p[0:tall, at:end] = y[:, NB:]
        left = left_terms(p[:, at:end])
        if not last:
            terms[y_rows(c, k) : y_rows(c, k) + tall, :] = three_terms(y[:, :NB])
        for b in range(owner(k), c):
            skip = max(k + 1 - STARTS[b], 0) * NB
            if skip < HEIGHTS[b] * NB:
                wait(("terms", b))
                cols = slice(STARTS[b] * NB + skip, (STARTS[b] + HEIGHTS[b]) * NB)
                right = right_six(held[b][y_rows(b, k) + skip : y_rows(b, k) + HEIGHTS[b] * NB, :])
                p[0:tall, cols] -= by_rows(left[0:tall], right)
        p[:, done:] -= by_rows(left, right_terms(y[:, :NB]))
    for i in range(HEIGHTS[c]):
        at, end = done + i * NB, done + (i + 1) * NB
        low, scl = eliminate([p[i * NB + r : i * NB + r + SUB, at:end] for r in range(0, NB, SUB)])
        for r in range(NB // SUB):
            ef[i, r * SUB : (r + 1) * SUB, :] = low[r]
            ef[i, NB + r * SUB : NB + (r + 1) * SUB, :] = scl[r]
        if not last:
            terms[i * 2 * NB : (i + 1) * 2 * NB, :] = three_terms(ef[i])
        both = right_terms(ef[i])
        rest = (i + 1) * NB
        y = by_rows(left_terms(p[rest:, at:end]), both)
        p[rest:, at:end] = y[:, NB:]
        if rest < tall:
            if not last:
                top = y_rows(c, STARTS[c] + i)
                terms[top : top + rest, :] = jnp.zeros((rest, 3 * NB), jnp.bfloat16)
                terms[top + rest : top + tall, :] = three_terms(y[0 : tall - rest, :NB])
            p[rest:, end:] -= by_rows(left_terms(y[:, NB:]), right_terms(y[0 : tall - rest, :NB]))
    if not last:
        x_out[...] = p[tall:, :]
        start("terms", terms, terms_out, sems.at[kept])
        start("w", p.at[0:tall, :], w_out, sems.at[kept + 1])
        wait("terms")
        wait("w")
        return
    for k in range(size // NB - 1, -1, -1):
        at, end = k * NB, (k + 1) * NB
        b = owner(k)
        i = k - STARTS[b]
        row = i * NB
        if b == c:
            e, w = ef[i, 0:NB, :], p[row : row + NB, 0:at]
        else:
            e = held[b][2 * row : 2 * row + NB, :].astype(jnp.float32)
            e = e[:, :NB] + e[:, NB : 2 * NB] + e[:, 2 * NB :]
            wait(("w", b))
            w = held[c + b][row : row + NB, 0:at]
        z = dot(p[tall:, at:end], e, ((1,), (0,)))
        p[tall:, at:end] = z
        if k:
            p[tall:, 0:at] -= dot(z, w, ((1,), (0,)))
    out_ref[...] = p[tall:, :] * scale


def panel(c, size, seqs, inputs, state):
    padded = -(-seqs // SUB) * SUB
    tall = HEIGHTS[c] * NB
    wide = STARTS[c] * NB + tall
    last = wide == size
    vmem, hbm = pl.BlockSpec(memory_space=pltpu.VMEM), pl.BlockSpec(memory_space=pltpu.HBM)
    shape = jax.ShapeDtypeStruct

    def terms_of(b):
        return y_rows(b, STARTS[b] + HEIGHTS[b] - 1), 3 * NB

    if last:
        outs, specs = [shape((padded, size), jnp.float32)], [vmem]
    else:
        outs = [
            shape((padded, wide), jnp.float32),
            shape(terms_of(c), jnp.bfloat16),
            shape((tall, wide), jnp.float32),
        ]
        specs = [vmem, hbm, hbm]
        if c == 0:
            outs, specs = [shape((padded + SUB, size), jnp.float32)] + outs, [vmem] + specs
    earlier = [terms for terms, _ in state] + ([w for _, w in state] if last else [])
    return pl.pallas_call(
        functools.partial(panel_kernel, c, size, seqs, padded),
        in_specs=([pl.BlockSpec(memory_space=pltpu.SMEM)] + [vmem] * 6 if c else [vmem]) + [hbm] * len(earlier),
        out_specs=specs,
        out_shape=outs,
        scratch_shapes=[
            pltpu.VMEM((tall + padded, wide), jnp.float32),
            pltpu.VMEM((HEIGHTS[c], 2 * NB, NB), jnp.float32),
            pltpu.VMEM(terms_of(0 if last else c), jnp.bfloat16),
            pltpu.SemaphoreType.DMA((len(earlier) + 2,)),
        ]
        + [pltpu.VMEM(x.shape, x.dtype) for x in earlier],
        compiler_params=pltpu.CompilerParams(vmem_limit_bytes=(60 if last else 40) << 20),
        cost_estimate=pl.CostEstimate(flops=1_200_000_000, bytes_accessed=4_000_000, transcendentals=0),
        name="panel%d" % c,
    )(*inputs, *earlier)


def score_kernel(side_ref, solved_ref, *refs):
    blocks, out_ref = refs[:-1], refs[-1]
    rows = solved_ref.shape[0]
    half = max(len(blocks) // 2, 1)
    count = blocks[0].shape[0]
    solved = jnp.concatenate(split(solved_ref[...]), axis=0)
    for i, block in enumerate(blocks):
        terms = by_rows(solved, block[...])
        low, high = half - 1 - i % half, (half + i % half) if len(blocks) > 1 else 0
        right_side = side_ref[0] if i < half else 1 - side_ref[0]
        at = pl.multiple_of((low + right_side * (high - low)) * count, LANES)
        out_ref[:, pl.ds(at, count)] = terms[0:rows] + terms[rows : 2 * rows] + terms[2 * rows :]


def score(side, solved, blocks):
    vmem = pl.BlockSpec(memory_space=pltpu.VMEM)
    count = len(blocks) * blocks[0].shape[0]
    return pl.pallas_call(
        score_kernel,
        in_specs=[pl.BlockSpec(memory_space=pltpu.SMEM)] + [vmem] * (1 + len(blocks)),
        out_specs=vmem,
        out_shape=jax.ShapeDtypeStruct((solved.shape[0], count), jnp.float32),
        name="score",
    )(side, solved, *blocks)


def after(x, *others):
    return lax.optimization_barrier((x,) + others)[0]


def inward(n):
    steps = [[(s, s + 1), (n - 1 - s, n - 2 - s)] for s in range(n // 2 - 1)]
    return steps + [[(n // 2 - 1, n // 2), (n // 2, n // 2 - 1)]] if n > 1 else []


def from_middle(x):
    n = lax.axis_size("dp")
    here = lax.axis_index("dp")
    for s in range(n // 2 - 2, -1, -1):
        got = lax.ppermute(x, "dp", [(s + 1, s), (n - 2 - s, n - 1 - s)])
        x = jnp.where((here == s) | (here == n - 1 - s), got, x)
    return x


SWAP = [(0, 1), (1, 0)]


def body(activations, out_grads, proj_in, proj_out, seq_lengths, fisher_prior, query_grads):
    tok_half = activations.shape[2]
    prior = fisher_prior[0, 0]
    size = prior.shape[0]
    seqs = lax.axis_size("dp")
    rep, dp = lax.axis_index("rep"), lax.axis_index("dp")
    count = len(HEIGHTS)
    steps = inward(seqs)

    def over_rep(c, gate):
        top, half = STARTS[c] * NB, HEIGHTS[c] * NB // 2
        wide = top + 2 * half
        array = prior if gate is None else after(prior, gate)
        other = lax.dynamic_slice(array, (top + (1 - rep) * half, 0), (half, wide))
        own = lax.dynamic_slice(array, (top + rep * half, 0), (half, wide))
        return own, lax.ppermute(other, "rep", SWAP)

    second = over_rep(1, None)
    place = jnp.stack([rep * tok_half, seq_lengths[0], dp]).astype(jnp.int32)
    first = project(place, seqs, activations, out_grads, proj_in, proj_out, fisher_prior)
    first = first + lax.ppermute(first, "rep", SWAP)
    swapped = came = first
    for i, step in enumerate(steps):
        first = first + lax.ppermute(first, "dp", step)
        if i == 0:
            came = first
    sums = [None, after(second[0] + second[1], came)]
    sums += [after(sum(over_rep(c, swapped)), came) for c in range(2, count)]

    def inwards(x, *gate):
        for step in steps[:-1]:
            x = x + after(lax.ppermute(x, "dp", step), *gate)
        return x

    inner = [None, inwards(sums[1], *sums[2:4])]
    aux, x_rows, *out = panel(0, size, seqs, [after(first, inner[1])], [])
    state, gates = [out], [aux]
    place = rep.astype(jnp.int32).reshape(1)

    inner.append(inwards(sums[2], gates[0]))
    for c in range(1, count):
        if c == 2:
            inner += [inwards(x, gates[1]) for x in sums[3:]]
        x = inner[c]
        got = lax.ppermute(x, "dp", steps[-1]) if steps else jnp.zeros_like(x)
        if c == 2:
            x = after(x, *inner[3:])
        got = after(got, gates[c - 1])
        others = [lax.ppermute(half, "rep", SWAP) for half in (x, got)]
        out = panel(c, size, seqs, [place, x, got, *others, aux, x_rows], state)
        gates.append(out[0])
        if c == 2:
            near = [after(query_grads[0, 0], out[0])]
            for step in steps[:-1]:
                near = near[:1] + [lax.ppermute(x, "dp", step) for x in near]
        if c == 3 and steps:
            near = list(lax.optimization_barrier((*near, out[0])))[:-1]
            near += [lax.ppermute(x, "dp", steps[-1]) for x in near]
        if c < count - 1:
            x_rows, *out = out
            state.append(out)
    side = (dp >= seqs // 2).astype(jnp.int32).reshape(1)
    scores = from_middle(score(side, out[0], near))
    mine = lax.dynamic_slice(scores, (dp, 0), (1, scores.shape[1]))
    if lax.axis_size("mod") == 2:
        return mine + lax.ppermute(mine, "mod", SWAP)
    return lax.psum(mine, "mod")


def solution(mesh):
    placed = (
        P("mod", ("grp", "dp"), "rep", None),
        P("mod", ("grp", "dp"), "rep", None),
        P("mod", None, None),
        P("mod", None, None),
        P(("grp", "dp")),
        P("mod", ("grp", "dp", "rep"), None, None),
        P("mod", "rep", "dp", None),
    )
    return jax.shard_map(
        body, mesh=mesh, in_specs=placed, out_specs=P(("grp", "dp"), "rep"), check_vma=False
    )
```

```python
import functools

import jax
import jax.numpy as jnp
from jax import lax
from jax.experimental import pallas as pl
from jax.experimental.pallas import tpu as pltpu
from jax.sharding import PartitionSpec as P

damping_frac = 0.01
NB = 128
LANES = 128
SUB = 8
HEIGHTS = (1, 2, 2, 2, 1)
STARTS = tuple(sum(HEIGHTS[:c]) for c in range(len(HEIGHTS)))
HIGH = lax.Precision.HIGHEST


def iota(shape, dim):
    return lax.broadcasted_iota(jnp.int32, shape, dim)


def dot(a, b, dims, precision=HIGH):
    return lax.dot_general(
        a, b, (dims, ((), ())), precision=precision, preferred_element_type=jnp.float32
    )


def split(x):
    one = x.astype(jnp.bfloat16)
    x = x - one.astype(jnp.float32)
    two = x.astype(jnp.bfloat16)
    three = (x - two.astype(jnp.float32)).astype(jnp.bfloat16)
    return one, two, three


def left_terms(x):
    one, two, three = split(x)
    return jnp.concatenate([one, one, two, two, one, three], axis=1)


def right_terms(x):
    one, two, three = split(x)
    return jnp.concatenate([one, two, one, two, three, one], axis=1)


def three_terms(x):
    return jnp.concatenate(split(x), axis=1)


def right_six(x):
    one, two, three = x[:, :NB], x[:, NB : 2 * NB], x[:, 2 * NB :]
    return jnp.concatenate([one, two, one, two, three, one], axis=1)


def by_rows(a, b):
    return dot(a, b, ((1,), (1,)), None)


def project_kernel(steps, seqs, place_ref, act_ref, grad_ref, pin_ref, pout_ref, prior_ref, out_ref, ins, outs, tr):
    step = pl.program_id(0)
    in_side = by_rows(act_ref[0, 0], pin_ref[0])
    out_side = by_rows(grad_ref[0, 0], pout_ref[0])
    block = prior_ref[0, 0]
    on_diag = iota(block.shape, 0) == iota(block.shape, 1)
    line = jnp.sum(jnp.where(on_diag, block, 0.0), axis=0, keepdims=True)
    line = sum(line[:, c : c + LANES] for c in range(0, block.shape[1], LANES))

    @pl.when(step == 0)
    def _():
        ins[...] = in_side
        outs[...] = out_side
        tr[...] = jnp.zeros_like(tr)
        tr[0:1, :] = line
        out_ref[out_ref.shape[0] - NB :, :] = block[0:NB, 0:NB]

    @pl.when(step > 0)
    def _():
        ins[...] += in_side
        outs[...] += out_side
        tr[0:1, :] += line

    @pl.when(step == steps - 1)
    def _():
        rank = ins.shape[1]
        fold = LANES // rank
        rows = rank // fold
        token = place_ref[0] + iota(outs.shape, 0)
        kept = jnp.where(token < place_ref[1], outs[...], 0.0)
        matrix = dot(kept, ins[...], ((0,), (0,)))
        matrix = jnp.concatenate([matrix] * fold, axis=1)
        o = iota((rank, LANES), 0)
        lane = iota((rank, LANES), 1)
        matrix = jnp.where(lax.rem(o, fold) == lane // rank, matrix, 0.0)
        pick = (iota((rows, rank), 1) // fold == iota((rows, rank), 0)).astype(jnp.float32)
        vector = dot(pick, matrix, ((1,), (0,)))
        for s in range(seqs):
            out_ref[s * rows : (s + 1) * rows, :] = jnp.where(place_ref[2] == s, vector, 0.0)
        out_ref[seqs * rows : (seqs + 1) * rows, :] = tr[...]


def project(place, seqs, activations, out_grads, proj_in, proj_out, fisher_prior):
    steps = 4
    tok, width = activations.shape[2:]
    rank = proj_in.shape[1]
    size = fisher_prior.shape[2]
    part, blk = width // steps, size // steps
    rows = size // LANES
    height = (seqs + 1) * rows + NB
    return pl.pallas_call(
        functools.partial(project_kernel, steps, seqs),
        grid=(steps,),
        in_specs=[
            pl.BlockSpec(memory_space=pltpu.SMEM),
            pl.BlockSpec((1, 1, tok, part), lambda i: (0, 0, 0, i)),
            pl.BlockSpec((1, 1, tok, part), lambda i: (0, 0, 0, i)),
            pl.BlockSpec((1, rank, part), lambda i: (0, 0, i)),
            pl.BlockSpec((1, rank, part), lambda i: (0, 0, i)),
            pl.BlockSpec((1, 1, blk, blk), lambda i: (0, 0, i, i)),
        ],
        out_specs=pl.BlockSpec((height, LANES), lambda i: (0, 0)),
        out_shape=jax.ShapeDtypeStruct((height, LANES), jnp.float32),
        scratch_shapes=[
            pltpu.VMEM((tok, rank), jnp.float32),
            pltpu.VMEM((tok, rank), jnp.float32),
            pltpu.VMEM((rows, LANES), jnp.float32),
        ],
        compiler_params=pltpu.CompilerParams(vmem_limit_bytes=60 << 20),
        name="project",
    )(place, activations, out_grads, proj_in, proj_out, fisher_prior)


def reciprocal(p):
    return pl.reciprocal(p, approx=True)


def spread(x, k):
    return jnp.broadcast_to(x[k : k + 1, :], x.shape)


def lanes_of(x, k):
    return jnp.broadcast_to(x[:, k : k + 1], x.shape)


def solve_group(s, sets):
    s = [list(row) for row in s]
    sets = [list(x) for x in sets]
    scaled = [[None] * SUB for _ in sets]
    pairs = []
    for k in range(0, SUB, 2):
        a, b, c = s[k][k], s[k + 1][k], s[k + 1][k + 1]
        r = reciprocal(a * c - b * b)
        rest = range(k + 2, SUB)
        m = {i: s[i][k] * c - s[i][k + 1] * b for i in rest}
        n = {i: s[i][k + 1] * a - s[i][k] * b for i in rest}
        for i in rest:
            for j in range(k + 2, i + 1):
                s[i][j] = s[i][j] - (m[i] * s[j][k] + n[i] * s[j][k + 1]) * r
        m = {i: m[i] * r for i in rest}
        n = {i: n[i] * r for i in rest}
        for x, y in zip(sets, scaled):
            y[k], y[k + 1] = (c * x[k] - b * x[k + 1]) * r, (a * x[k + 1] - b * x[k]) * r
            for i in rest:
                x[i] = x[i] - (m[i] * x[k] + n[i] * x[k + 1])
        pairs.append((m, n))
    return sets, scaled, pairs


def back_group(w, pairs):
    w = list(w)
    for k in range(SUB - 4, -1, -2):
        m, n = pairs[k // 2]
        for i in range(SUB - 2, k, -2):
            w[k] = w[k] - (m[i] * w[i] + m[i + 1] * w[i + 1])
            w[k + 1] = w[k + 1] - (n[i] * w[i] + n[i + 1] * w[i + 1])
    return w


def less_products(x, a, b):
    early = (a[0] * b[0] + a[1] * b[1]) + (a[2] * b[2] + a[3] * b[3])
    return (x - early) - (a[4] * b[4] + a[5] * b[5]) - (a[6] * b[6] + a[7] * b[7])


def eliminate(rows):
    groups = len(rows)
    rows = list(rows)
    sub = iota((SUB, LANES), 0)
    lane = iota((SUB, LANES), 1)
    lower, scaled_rows = [], []
    cols = [lanes_of(rows[0], j) for j in range(SUB)]
    for g in range(groups):
        first = g * SUB
        here = (lane >= first) & (lane < first + SUB)
        unit = (lane - first == sub).astype(jnp.float32)
        s = [[spread(cols[j], i) for j in range(i + 1)] for i in range(SUB)]
        work = jnp.where(here, unit, rows[g])
        lower.append(jnp.where(lane < first + SUB, work, 0.0))
        near = list(range(g + 1, min(g + 3, groups)))
        sets = [[lanes_of(rows[h], first + j) for j in range(SUB)] for h in near]
        if near:
            ahead = [lanes_of(rows[g + 1], first + SUB + j) for j in range(SUB)]
        sets, scaled, pairs = solve_group(s, sets + [[spread(work, i) for i in range(SUB)]])
        if near:
            cols = [less_products(ahead[j], sets[0], [spread(d, j) for d in scaled[0]]) for j in range(SUB)]
        for h, x in zip(near, sets):
            rows[h] = less_products(jnp.where(here, 0.0, rows[h]), x, scaled[-1])
        picks = back_group(scaled[-1], pairs)
        work = picks[0]
        for i in range(1, SUB):
            work = jnp.where(sub == i, picks[i], work)
        scaled_rows.append(jnp.where(lane < first + SUB, work, 0.0))
        for h in range(g + 3, groups):
            x = [lanes_of(rows[h], first + j) for j in range(SUB)]
            rows[h] = less_products(jnp.where(here, 0.0, rows[h]), x[::-1], picks[::-1])
    return lower, scaled_rows


def owner(k):
    return max(b for b in range(len(STARTS)) if STARTS[b] <= k)


def y_rows(b, k):
    return HEIGHTS[b] * 2 * NB + k * HEIGHTS[b] * NB


def panel_kernel(c, size, seqs, padded, *refs):
    refs = list(refs)
    tall, done = HEIGHTS[c] * NB, STARTS[c] * NB
    wide = done + tall
    last = wide == size
    waits = {}

    def start(name, source, target, sem):
        waits[name] = pltpu.make_async_copy(source, target, sem)
        waits[name].start()

    def wait(name):
        if name in waits:
            waits.pop(name).wait()

    if c == 0:
        first_ref = refs.pop(0)
        head = first_ref.shape[0] - NB
        rows = size // LANES
    else:
        place_ref, half_ref, got_ref, half_other_ref, got_other_ref, aux_ref, x_ref = refs[:7]
        del refs[:7]
    kept = c + (c if last else 0)
    given = refs[:kept]
    del refs[:kept]
    if last:
        out_ref = refs.pop(0)
    else:
        if c == 0:
            aux_ref = refs.pop(0)
        x_out, terms_out, w_out = refs[:3]
        del refs[:3]
    p, ef, terms, sems = refs[:4]
    held = refs[4:]
    for b in range(kept):
        start(("terms", b) if b < c else ("w", b - c), given[b], held[b], sems.at[b])

    if c == 0:
        if padded > seqs:
            aux_ref[seqs:padded, :] = jnp.zeros((padded - seqs, size), jnp.float32)
        for r in range(seqs * rows):
            at = r % rows * LANES
            aux_ref[r // rows : r // rows + 1, at : at + LANES] = first_ref[r : r + 1, :]
        v = aux_ref[0:padded, :]
        trace = jnp.sum(first_ref[seqs * rows : head, :]) + jnp.sum(v * v)
        aux_ref[padded:, :] = size / jnp.broadcast_to(trace, (SUB, size))
    scale = aux_ref[padded : padded + 1, :]
    one, two, three = split(aux_ref[0:padded, 0:wide])
    outer_left = jnp.concatenate([x[:, done:] for x in (one, one, two, two, one, three)], axis=0)
    outer_right = jnp.concatenate([one, two, one, two, three, one], axis=0)
    if c == 0:
        p[0:NB, :] = first_ref[head:, :]
    else:
        rep, half = place_ref[0], tall // 2
        p[pl.ds(pl.multiple_of(rep * half, half), half), :] = half_ref[...] + got_ref[...]
        p[pl.ds(pl.multiple_of((1 - rep) * half, half), half), :] = half_other_ref[...] + got_other_ref[...]
    outer = dot(outer_left, outer_right, ((0,), (0,)), None)
    eye = iota((tall, wide), 0) + done == iota((tall, wide), 1)
    p[0:tall, :] = (p[0:tall, :] + outer) * scale[:, 0:wide] + jnp.where(eye, damping_frac, 0.0)
    if c:
        p[tall:, 0:done] = x_ref[...]
    p[tall:, done:] = aux_ref[0:padded, done:wide]

    for k in range(STARTS[c]):
        at, end = k * NB, (k + 1) * NB
        b = owner(k)
        wait(("terms", b))
        both = right_six(held[b][(k - STARTS[b]) * 2 * NB : (k - STARTS[b] + 1) * 2 * NB, :])
        y = by_rows(left_terms(p[0:tall, at:end]), both)
        p[0:tall, at:end] = y[:, NB:]
        left = left_terms(p[:, at:end])
        if not last:
            terms[y_rows(c, k) : y_rows(c, k) + tall, :] = three_terms(y[:, :NB])
        for b in range(owner(k), c):
            skip = max(k + 1 - STARTS[b], 0) * NB
            if skip < HEIGHTS[b] * NB:
                wait(("terms", b))
                cols = slice(STARTS[b] * NB + skip, (STARTS[b] + HEIGHTS[b]) * NB)
                right = right_six(held[b][y_rows(b, k) + skip : y_rows(b, k) + HEIGHTS[b] * NB, :])
                p[0:tall, cols] -= by_rows(left[0:tall], right)
        p[:, done:] -= by_rows(left, right_terms(y[:, :NB]))
    for i in range(HEIGHTS[c]):
        at, end = done + i * NB, done + (i + 1) * NB
        low, scl = eliminate([p[i * NB + r : i * NB + r + SUB, at:end] for r in range(0, NB, SUB)])
        for r in range(NB // SUB):
            ef[i, r * SUB : (r + 1) * SUB, :] = low[r]
            ef[i, NB + r * SUB : NB + (r + 1) * SUB, :] = scl[r]
        if not last:
            terms[i * 2 * NB : (i + 1) * 2 * NB, :] = three_terms(ef[i])
        both = right_terms(ef[i])
        rest = (i + 1) * NB
        y = by_rows(left_terms(p[rest:, at:end]), both)
        p[rest:, at:end] = y[:, NB:]
        if rest < tall:
            if not last:
                top = y_rows(c, STARTS[c] + i)
                terms[top : top + rest, :] = jnp.zeros((rest, 3 * NB), jnp.bfloat16)
                terms[top + rest : top + tall, :] = three_terms(y[0 : tall - rest, :NB])
            p[rest:, end:] -= by_rows(left_terms(y[:, NB:]), right_terms(y[0 : tall - rest, :NB]))
    if not last:
        x_out[...] = p[tall:, :]
        start("terms", terms, terms_out, sems.at[kept])
        start("w", p.at[0:tall, :], w_out, sems.at[kept + 1])
        wait("terms")
        wait("w")
        return
    for k in range(size // NB - 1, -1, -1):
        at, end = k * NB, (k + 1) * NB
        b = owner(k)
        i = k - STARTS[b]
        row = i * NB
        if b == c:
            e, w = ef[i, 0:NB, :], p[row : row + NB, 0:at]
        else:
            e = held[b][2 * row : 2 * row + NB, :].astype(jnp.float32)
            e = e[:, :NB] + e[:, NB : 2 * NB] + e[:, 2 * NB :]
            wait(("w", b))
            w = held[c + b][row : row + NB, 0:at]
        z = dot(p[tall:, at:end], e, ((1,), (0,)))
        p[tall:, at:end] = z
        if k:
            p[tall:, 0:at] -= dot(z, w, ((1,), (0,)))
    out_ref[...] = p[tall:, :] * scale


def panel(c, size, seqs, inputs, state):
    padded = -(-seqs // SUB) * SUB
    tall = HEIGHTS[c] * NB
    wide = STARTS[c] * NB + tall
    last = wide == size
    vmem, hbm = pl.BlockSpec(memory_space=pltpu.VMEM), pl.BlockSpec(memory_space=pltpu.HBM)
    shape = jax.ShapeDtypeStruct

    def terms_of(b):
        return y_rows(b, STARTS[b] + HEIGHTS[b] - 1), 3 * NB

    if last:
        outs, specs = [shape((padded, size), jnp.float32)], [vmem]
    else:
        outs = [
            shape((padded, wide), jnp.float32),
            shape(terms_of(c), jnp.bfloat16),
            shape((tall, wide), jnp.float32),
        ]
        specs = [vmem, hbm, hbm]
        if c == 0:
            outs, specs = [shape((padded + SUB, size), jnp.float32)] + outs, [vmem] + specs
    earlier = [terms for terms, _ in state] + ([w for _, w in state] if last else [])
    return pl.pallas_call(
        functools.partial(panel_kernel, c, size, seqs, padded),
        in_specs=([pl.BlockSpec(memory_space=pltpu.SMEM)] + [vmem] * 6 if c else [vmem]) + [hbm] * len(earlier),
        out_specs=specs,
        out_shape=outs,
        scratch_shapes=[
            pltpu.VMEM((tall + padded, wide), jnp.float32),
            pltpu.VMEM((HEIGHTS[c], 2 * NB, NB), jnp.float32),
            pltpu.VMEM(terms_of(0 if last else c), jnp.bfloat16),
            pltpu.SemaphoreType.DMA((len(earlier) + 2,)),
        ]
        + [pltpu.VMEM(x.shape, x.dtype) for x in earlier],
        compiler_params=pltpu.CompilerParams(vmem_limit_bytes=(60 if wide + 2 * NB > size else 40) << 20),
        cost_estimate=pl.CostEstimate(flops=1_200_000_000, bytes_accessed=4_000_000, transcendentals=0),
        name="panel%d" % c,
    )(*inputs, *earlier)


def score_kernel(count, side_ref, solved_ref, *refs):
    sides, out_ref = refs[:-1], refs[-1]
    rows = solved_ref.shape[0]
    half = sides[0].shape[0] // count
    solved = jnp.concatenate(split(solved_ref[...]), axis=0)
    for i, side in enumerate(sides):
        right_side = side_ref[0] if i == 0 else 1 - side_ref[0]
        for r in range(half):
            terms = by_rows(solved, side[r * count : (r + 1) * count, :])
            low, high = half - 1 - r, (half + r if len(sides) > 1 else 0)
            at = pl.multiple_of((low + right_side * (high - low)) * count, LANES)
            out_ref[:, pl.ds(at, count)] = terms[0:rows] + terms[rows : 2 * rows] + terms[2 * rows :]


def score(count, side, solved, sides):
    vmem = pl.BlockSpec(memory_space=pltpu.VMEM)
    total = len(sides) * sides[0].shape[0]
    return pl.pallas_call(
        functools.partial(score_kernel, count),
        in_specs=[pl.BlockSpec(memory_space=pltpu.SMEM)] + [vmem] * (1 + len(sides)),
        out_specs=vmem,
        out_shape=jax.ShapeDtypeStruct((solved.shape[0], total), jnp.float32),
        name="score",
    )(side, solved, *sides)


def after(x, *others):
    return lax.optimization_barrier((x,) + others)[0]


def inward(n):
    steps = [[(s, s + 1), (n - 1 - s, n - 2 - s)] for s in range(n // 2 - 1)]
    return steps + [[(n // 2 - 1, n // 2), (n // 2, n // 2 - 1)]] if n > 1 else []


def from_middle(x):
    n = lax.axis_size("dp")
    here = lax.axis_index("dp")
    for s in range(n // 2 - 2, -1, -1):
        got = lax.ppermute(x, "dp", [(s + 1, s), (n - 2 - s, n - 1 - s)])
        x = jnp.where((here == s) | (here == n - 1 - s), got, x)
    return x


SWAP = [(0, 1), (1, 0)]


def body(activations, out_grads, proj_in, proj_out, seq_lengths, fisher_prior, query_grads):
    tok_half = activations.shape[2]
    prior = fisher_prior[0, 0]
    size = prior.shape[0]
    seqs = lax.axis_size("dp")
    rep, dp = lax.axis_index("rep"), lax.axis_index("dp")
    count = len(HEIGHTS)
    steps = inward(seqs)

    def over_rep(c, gate):
        top, half = STARTS[c] * NB, HEIGHTS[c] * NB // 2
        wide = top + 2 * half
        array = prior if gate is None else after(prior, gate)
        other = lax.dynamic_slice(array, (top + (1 - rep) * half, 0), (half, wide))
        own = lax.dynamic_slice(array, (top + rep * half, 0), (half, wide))
        return own, lax.ppermute(other, "rep", SWAP)

    second = over_rep(1, None)
    place = jnp.stack([rep * tok_half, seq_lengths[0], dp]).astype(jnp.int32)
    first = project(place, seqs, activations, out_grads, proj_in, proj_out, fisher_prior)
    first = first + lax.ppermute(first, "rep", SWAP)
    swapped = came = first
    for i, step in enumerate(steps):
        first = first + lax.ppermute(first, "dp", step)
        if i == 0:
            came = first
    sums = [None, after(second[0] + second[1], came)]
    sums += [after(sum(over_rep(c, swapped)), came) for c in range(2, count)]

    def inwards(x, *gate):
        for step in steps[:-1]:
            x = x + after(lax.ppermute(x, "dp", step), *gate)
        return x

    inner = [None, inwards(sums[1], *sums[2:4])]
    aux, x_rows, *out = panel(0, size, seqs, [after(first, inner[1])], [])
    state, gates = [out], [aux]
    place = rep.astype(jnp.int32).reshape(1)

    inner.append(inwards(sums[2], gates[0]))
    for c in range(1, count):
        if c == 2:
            inner += [inwards(x, gates[1]) for x in sums[3:]]
        x = inner[c]
        got = lax.ppermute(x, "dp", steps[-1]) if steps else jnp.zeros_like(x)
        if c == 2:
            x = after(x, *inner[3:])
        got = after(got, gates[c - 1])
        others = [lax.ppermute(half, "rep", SWAP) for half in (x, got)]
        out = panel(c, size, seqs, [place, x, got, *others, aux, x_rows], state)
        gates.append(out[0])
        if c == 2:
            near = [after(query_grads[0, 0], out[0])]
            for step in steps[:-1]:
                near = near[:1] + [lax.ppermute(x, "dp", step) for x in near]
        if c == 3 and steps:
            near = jnp.concatenate(near[:1] + [after(x, out[0]) for x in near[1:]], axis=0)
            near = [near, lax.ppermute(near, "dp", steps[-1])]
        if c < count - 1:
            x_rows, *out = out
            state.append(out)
    side = (dp >= seqs // 2).astype(jnp.int32).reshape(1)
    scores = from_middle(score(query_grads.shape[2], side, out[0], near))
    mine = lax.dynamic_slice(scores, (dp, 0), (1, scores.shape[1]))
    if lax.axis_size("mod") == 2:
        return mine + lax.ppermute(mine, "mod", SWAP)
    return lax.psum(mine, "mod")


def solution(mesh):
    placed = (
        P("mod", ("grp", "dp"), "rep", None),
        P("mod", ("grp", "dp"), "rep", None),
        P("mod", None, None),
        P("mod", None, None),
        P(("grp", "dp")),
        P("mod", ("grp", "dp", "rep"), None, None),
        P("mod", "rep", "dp", None),
    )
    return jax.shard_map(
        body, mesh=mesh, in_specs=placed, out_specs=P(("grp", "dp"), "rep"), check_vma=False
    )
```
